128 devices in a mesh: seq: 8 (over y, core), tensor: 16 (over x, z).
Axes of the slice: x: 4, y: 4, z: 4, core: 2. Of those that a mesh axis runs over, the one named last changes fastest.
Arguments:
- tokens: bfloat16 [16384, 4096], P('seq', 'tensor'), may hold values from -6 to 6
- w_query: bfloat16 [4096, 4096], P(None, 'tensor'), may hold values from -0.09375 to 0.09375
- w_key: bfloat16 [4096, 4096], P(None, 'tensor'), may hold values from -0.09375 to 0.09375
- w_value: bfloat16 [4096, 4096], P(None, 'tensor'), may hold values from -0.09375 to 0.09375
- w_output: bfloat16 [4096, 4096], P('tensor'), may hold values from -0.09375 to 0.09375
Outputs:
- mixed: bfloat16 [16384, 4096], P('seq', 'tensor')
The draws below stay inside these ranges and needn't reach their ends.
All inputs are finite; a program needn't handle non-finite values.
Results may differ from the reference program's by a relative error of at most 0.023.
Values may be sent and summed in bfloat16 or wider, within the bound.
A program may use at most 128 MiB of HBM per device.

```python
import math
import jax
import jax.numpy as jnp
from jax import lax

D = 4096
H = 32
DH = 128
BLOCK = 256
LENGTH = 16384


def levels(stream_key, extent, split, smallest, high):
    loudness = 1.0
    for dim, parts in split:
        heights = jax.random.uniform(jax.random.fold_in(jax.random.fold_in(stream_key, 6), dim), (parts,), jnp.float32, smallest / len(split), high / len(split))
        loudness = loudness * jnp.repeat(jnp.exp(heights), extent[dim] // parts).reshape((-1,) + (1,) * (len(extent) - 1 - dim))
    return loudness


def normal_values(own_key, shape, scale, most, shards=(), held_as=jnp.bfloat16):
    values = jax.random.normal(own_key, shape, jnp.float32) * scale
    if len(shards) > 0:
        values = levels(own_key, shape, shards, -0.22, 0.18) * values
    return jnp.clip(values, min=-most, max=most).astype(held_as)


def setup_inputs(seed: int = 0) -> dict:
    keys = jax.random.split(jax.random.key(seed), 6)
    return {
        "tokens": normal_values(keys[0], (LENGTH, D), 1.0, 6.0, ((0, 8), (1, 16))),
        "w_query": normal_values(keys[1], (D, H * DH), D ** -0.5, 0.09375, ((1, 16),)),
        "w_key": normal_values(keys[2], (D, H * DH), D ** -0.5, 0.09375, ((1, 16),)),
        "w_value": normal_values(keys[3], (D, H * DH), D ** -0.5, 0.09375, ((1, 16),)),
        "w_output": normal_values(keys[4], (H * DH, D), (H * DH) ** -0.5, 0.09375, ((0, 16),)),
    }


def reference(tokens, w_query, w_key, w_value, w_output):
    query = jnp.dot(tokens, w_query, preferred_element_type=jnp.float32).astype(jnp.bfloat16)
    key_all = jnp.dot(tokens, w_key, preferred_element_type=jnp.float32).astype(jnp.bfloat16)
    value_all = jnp.dot(tokens, w_value, preferred_element_type=jnp.float32).astype(jnp.bfloat16)
    block_count = LENGTH // BLOCK
    att_scale = 1.0 / math.sqrt(DH * LENGTH)
    causal_mask = jnp.arange(BLOCK)[:, None] >= jnp.arange(BLOCK)[None, :]

    def one_head(head_index):
        first_col = (head_index * DH).astype(jnp.int32)
        q_head = lax.dynamic_slice_in_dim(query, first_col, DH, 1).reshape(block_count, BLOCK, DH).astype(jnp.float32)
        k_head = lax.dynamic_slice_in_dim(key_all, first_col, DH, 1).reshape(block_count, BLOCK, DH).astype(jnp.float32)
        v_head = lax.dynamic_slice_in_dim(value_all, first_col, DH, 1).reshape(block_count, BLOCK, DH).astype(jnp.float32)
        block_states = jnp.einsum('nbd,nbe->nde', k_head, v_head)
        running = jnp.cumsum(block_states, axis=0)
        before = jnp.concatenate([jnp.zeros((1, DH, DH), jnp.float32), running[:-1]], axis=0)
        before_low = lax.optimization_barrier(before.astype(jnp.bfloat16)).astype(jnp.float32)
        inter = jnp.einsum('nbd,nde->nbe', q_head, before_low)
        scores = jnp.einsum('nbd,ncd->nbc', q_head, k_head)
        scores = jnp.where(causal_mask[None], scores, jnp.float32(0.0))
        scores_low = lax.optimization_barrier(scores.astype(jnp.bfloat16)).astype(jnp.float32)
        intra = jnp.einsum('nbc,nce->nbe', scores_low, v_head)
        return ((inter + intra) * att_scale).astype(jnp.bfloat16).reshape(LENGTH, DH)
    head_outputs = lax.map(one_head, jnp.arange(H, dtype=jnp.int32))
    attended = jnp.transpose(head_outputs, (1, 0, 2)).reshape(LENGTH, H * DH)
    return jnp.dot(attended, w_output, preferred_element_type=jnp.float32).astype(jnp.bfloat16)
```

```python
import math

import jax
import jax.numpy as jnp
from jax import lax
from jax.experimental import pallas as pl
from jax.experimental.pallas import tpu as pltpu
from jax.sharding import PartitionSpec as P

DH = 128
BLOCK = 256
BF = jnp.bfloat16
F32 = jnp.float32
NB = 8
RX = 160
RZ = BLOCK - RX
HZ = RZ // 2
OC = 128
NO = 8
FEAT = 256
SIB = 15
SIB3 = 7


def remote(src, dst, send, recv, device):
    return pltpu.make_async_remote_copy(
        src_ref=src, dst_ref=dst, send_sem=send, recv_sem=recv,
        device_id=device, device_id_type=pl.DeviceIdType.MESH,
    )


def kernel(scale, tok, wq, wk, wv, wo, out,
           xg, w, q, qkv, intra, st, run, tot, carry, low, attn, ag, wog, outb,
           pre_s, pre_r, w_l, w1_s, w1_r, w2_s, w2_r, o1_s, o1_r, o2_s, o2_r, o3_s, o3_r,
           g_s, g_r, t_s, t_r, a_s, a_r, r_s, r_r):
    div, rem = lax.div, lax.rem
    seq, ten = lax.axis_index("seq"), lax.axis_index("tensor")
    y, c, x, z = div(seq, 2), rem(seq, 2), div(ten, 4), rem(ten, 4)
    half, xi = div(x, 2), rem(x, 2)
    xn, xc = x + 1 - 2 * xi, 3 - x
    mine = c == half
    other = jnp.logical_not(mine)
    shard = 2 * y + half
    zp, zm, z2 = rem(z + 1, 4), rem(z + 3, 4), rem(z + 2, 4)

    def at(y_, c_, x_, z_):
        return (2 * y_ + c_, 4 * x_ + z_)

    d_xn, d_zp, d_zm = at(y, c, xn, z), at(y, c, x, zp), at(y, c, x, zm)
    d_sib, d_part = at(y, 1 - c, x, z), at(y, 1 - c, xc, z)

    def col(x_, z_, own=True):
        natural = mine if own else other
        return pl.multiple_of((jnp.where(natural, x_, 3 - x_) * 4 + z_) * FEAT, FEAT)

    places = ((x, z), (xn, z), (x, zm), (x, zp), (xn, zm), (xn, zp), (x, z2), (xn, z2))
    cols = [col(*p) for p in places]
    sib_cols = [col(*p, own=False) for p in places]
    c_own, c_x, c_m, c_p, c_xm, c_xp, c_2, c_x2 = cols

    barrier = pltpu.get_barrier_semaphore()
    peers = [d_sib, d_part, at(y, 1 - c, xc + 1 - 2 * rem(xc, 2), z)]
    for d in (1, 2, 3):
        peers += [at(y, c, x, rem(z + d, 4)), at(y, c, rem(x + d, 4), z),
                  at(rem(y + d, 4), c, x, z), at(rem(y + d, 4), c, xc, z)]
    for peer in peers:
        pl.semaphore_signal(barrier, inc=1, device_id=peer, device_id_type=pl.DeviceIdType.MESH)
    pl.semaphore_wait(barrier, len(peers))

    t_col = pl.multiple_of(ten * FEAT, FEAT)
    p_col = pl.multiple_of((4 * xc + z) * FEAT, FEAT)
    w_hbm = (wq, wk, wv)
    quarter = pl.ds(pl.multiple_of(y * 1024, 1024), 1024)

    def block_rows(r):
        return pl.ds(pl.multiple_of(r * BLOCK, BLOCK), BLOCK)

    def tok_local(r):
        return pltpu.make_async_copy(tok.at[block_rows(r)], xg.at[r, :, pl.ds(t_col, FEAT)], pre_r.at[r])

    def tok_remote(r):
        return remote(tok.at[block_rows(r)], xg.at[r, :, pl.ds(t_col, FEAT)], pre_s.at[r], pre_r.at[r], d_part)

    def tok_wait(r):
        slot = xg.at[r, :, pl.ds(c_own, FEAT)]
        pltpu.make_async_copy(tok.at[block_rows(r)], slot, pre_r.at[r]).wait()

    def w_local(n):
        return pltpu.make_async_copy(w_hbm[n], w.at[n], w_l.at[n])

    def w_first(n):
        return remote(w_hbm[n].at[quarter], w.at[n, quarter], w1_s.at[n], w1_r.at[n], d_part)

    def w_second(n, d):
        return remote(w.at[n, quarter], w.at[n, quarter], w2_s.at[n, d], w2_r.at[n, d],
                      at(rem(y + d, 4), c, x, z))

    o_cols = pl.ds(pl.multiple_of(rem(y, 2) * DH, DH), DH)
    o_blk = div(y, 2)

    def o_source(z_):
        return wo.at[:, pl.ds(pl.multiple_of(((2 * c + o_blk) * 4 + z_) * FEAT + rem(y, 2) * DH, DH), DH)]

    o_mine = wog.at[o_blk, pl.ds(pl.multiple_of(ten * FEAT, FEAT), FEAT), o_cols]

    def o_first(d):
        if d == 0:
            return pltpu.make_async_copy(o_source(z), o_mine, o1_r.at[0])
        to = rem(z + d, 4)
        return remote(o_source(to), o_mine, o1_s.at[d], o1_r.at[d], at(y, c, x, to))

    def o_second(d):
        part = wog.at[o_blk, pl.ds(pl.multiple_of(x * 1024, 1024), 1024), o_cols]
        return remote(part, part, o2_s.at[d], o2_r.at[d], at(y, c, rem(x + d, 4), z))

    def o_third(d):
        part = wog.at[o_blk, :, o_cols]
        return remote(part, part, o3_s.at[d], o3_r.at[d], at(rem(y + d, 4), c, x, z))

    @pl.when(mine)
    def _():
        def start(r, _):
            tok_local(r).start()
            return 0
        lax.fori_loop(0, NB, start, 0)
        for n in range(3):
            w_local(n).start()

    def send_inputs(k):
        for step in range(4):
            @pl.when(jnp.logical_and(other, k == step))
            def _(step=step):
                tok_remote(2 * step).start()
                tok_remote(2 * step + 1).start()
                if step < 3:
                    w_first(step).start()
        for step in range(3):
            @pl.when(jnp.logical_and(other, k == step + 2))
            def _(step=step):
                w_first(step).wait_recv()
                for d in (1, 2, 3):
                    w_second(step, d).start()

        @pl.when(k == 1)
        def _():
            for d in range(4):
                o_first(d).start()

        @pl.when(k == 4)
        def _():
            o_first(0).wait()
            for d in (1, 2, 3):
                o_first(d).wait_recv()
            for d in (1, 2, 3):
                o_second(d).start()

        @pl.when(k == 7)
        def _():
            for d in (1, 2, 3):
                o_second(d).wait_recv()
            for d in (1, 2, 3):
                o_third(d).start()

    ALL, XF, ZF = pl.ds(0, BLOCK), pl.ds(0, RX), pl.ds(RX, RZ)
    Z1, Z2 = pl.ds(RX, HZ), pl.ds(RX + HZ, HZ)

    def gather(r, k, rows, column, device=None):
        slot = xg.at[r, rows, pl.ds(column, FEAT)]
        return remote(slot, slot, g_s.at[r, k], g_r.at[r, k], d_sib if device is None else device)

    def to_sibling(r, piece):
        gather(r, SIB + piece, ALL, cols[piece]).start()

    def hop0(r):
        tok_wait(r)
        gather(r, 0, XF, c_own, d_xn).start()
        gather(r, 8, ZF, c_own, d_zp).start()
        gather(r, 9, ZF, c_own, d_zm).start()
        gather(r, 1, XF, c_own, d_zp).start()
        gather(r, 2, XF, c_own, d_zm).start()
        gather(r, 7, ZF, c_own, d_xn).start()
        to_sibling(r, 0)

    def hop1(r):
        gather(r, 0, XF, c_x).wait_recv()
        gather(r, 3, XF, c_x, d_zp).start()
        gather(r, 4, XF, c_x, d_zm).start()
        gather(r, 8, ZF, c_m).wait_recv()
        gather(r, 10, Z1, c_m, d_zp).start()
        gather(r, 12, ZF, c_m, d_xn).start()
        gather(r, 9, ZF, c_p).wait_recv()
        gather(r, 11, Z2, c_p, d_zm).start()
        gather(r, 13, ZF, c_p, d_xn).start()
        gather(r, 1, XF, c_m).wait_recv()
        gather(r, 5, XF, c_m, d_zp).start()
        to_sibling(r, 2)
        gather(r, 2, XF, c_p).wait_recv()
        to_sibling(r, 3)
        gather(r, 7, ZF, c_x).wait_recv()
        to_sibling(r, 1)

    def hop2(r):
        gather(r, 4, XF, c_xp).wait_recv()
        gather(r, 6, XF, c_xp, d_zm).start()
        gather(r, 10, Z1, c_2).wait_recv()
        gather(r, 11, Z2, c_2).wait_recv()
        gather(r, 14, ZF, c_2, d_xn).start()
        gather(r, 3, XF, c_xm).wait_recv()
        gather(r, 12, ZF, c_xm).wait_recv()
        to_sibling(r, 4)
        gather(r, 13, ZF, c_xp).wait_recv()
        to_sibling(r, 5)

    def hop3(r):
        gather(r, 5, XF, c_2).wait_recv()
        to_sibling(r, 6)
        gather(r, 6, XF, c_x2).wait_recv()
        gather(r, 14, ZF, c_x2).wait_recv()
        to_sibling(r, 7)

    def heads(n):
        return slice(n * DH, (n + 1) * DH)

    def state_copy(to):
        to_y, to_half = div(to, 2), rem(to, 2)
        to_x = jnp.where(to_half == half, x, xc)
        return remote(tot, carry.at[shard], t_s.at[to], t_r.at[shard], at(to_y, c, to_x, z))

    def block(r, _):
        for piece in range(8):
            gather(r, SIB + piece, ALL, sib_cols[piece]).wait_recv()

        def project(n, _):
            qkv[n] = jnp.dot(xg[r], w[n], preferred_element_type=F32).astype(BF)
            return 0
        lax.fori_loop(0, 3, project, 0)
        q[r] = qkv[0]
        for n in range(2):
            total = run[n]
            st[r, n] = total
            run[n] = total + lax.dot_general(
                qkv[1, :, heads(n)], qkv[2, :, heads(n)], (((0,), (0,)), ((), ())), preferred_element_type=F32)

        @pl.when(r == NB - 1)
        def _():
            tot[...] = run[...].astype(BF)

            def send(to, _):
                state_copy(to).start()
                return 0
            lax.fori_loop(shard + 1, 8, send, 0)

        causal = (lax.broadcasted_iota(jnp.int32, (BLOCK, BLOCK), 0)
                  >= lax.broadcasted_iota(jnp.int32, (BLOCK, BLOCK), 1))
        for n in range(2):
            scores = lax.dot_general(
                qkv[0, :, heads(n)], qkv[1, :, heads(n)], (((1,), (1,)), ((), ())), preferred_element_type=F32)
            scores = jnp.where(causal, scores, 0.0).astype(BF)
            intra[r, :, heads(n)] = jnp.dot(scores, qkv[2, :, heads(n)], preferred_element_type=F32)
        return 0

    run[...] = jnp.zeros_like(run)

    def round1(k, _):
        send_inputs(k)

        @pl.when(k < NB)
        def _():
            hop0(k)

        @pl.when(jnp.logical_and(k >= 1, k < NB + 1))
        def _():
            hop1(k - 1)

        @pl.when(jnp.logical_and(k >= 2, k < NB + 2))
        def _():
            hop2(k - 2)

        @pl.when(jnp.logical_and(k >= 3, k < NB + 3))
        def _():
            hop3(k - 3)

        @pl.when(jnp.logical_and(mine, k == 6))
        def _():
            for n in range(3):
                w_local(n).wait()

        @pl.when(jnp.logical_and(other, k == 6))
        def _():
            for n in range(3):
                for d in (1, 2, 3):
                    w_second(n, d).wait_recv()

        def done(k_):
            return jnp.maximum(jnp.minimum(k_ - 2, 2 * (k_ - 5)), 0)
        lax.fori_loop(done(k - 1), done(k), block, 0)
        return 0
    lax.fori_loop(0, NB + 3, round1, 0)

    run[...] = jnp.zeros_like(run)

    def add(k, _):
        remote(tot, carry.at[k], t_s.at[k], t_r.at[k], d_sib).wait_recv()
        run[...] += carry[k].astype(F32)
        return 0
    lax.fori_loop(0, shard, add, 0)

    def lower(r, _):
        low[r] = (st[r] + run[...]).astype(BF)
        return 0
    lax.fori_loop(0, NB, lower, 0)

    def attended(r, sub):
        rows = pl.ds(pl.multiple_of(sub * OC, OC), OC)
        parts = []
        for n in range(2):
            inter = jnp.dot(q[r, rows, heads(n)], low[r, n], preferred_element_type=F32)
            parts.append(((inter + intra[r, rows, heads(n)]) * scale).astype(BF))
        return jnp.concatenate(parts, axis=1)

    def spread(m, k, column, device=None):
        slot = ag.at[m, :, pl.ds(column, FEAT)]
        return remote(slot, slot, a_s.at[m, k], a_r.at[m, k], d_sib if device is None else device)

    def spread_sibling(m, piece):
        spread(m, SIB3 + piece, cols[piece]).start()

    def hand_over(m):
        return remote(attn.at[m], ag.at[m, :, pl.ds(c_own, FEAT)], a_s.at[m, 0], a_r.at[m, 0], d_xn)

    def turn0(m):
        r, sub = 2 * div(m, 2), rem(m, 2)
        ag[m, :, pl.ds(c_own, FEAT)] = attended(r + xi, sub)
        spread(m, 1, c_own, d_zp).start()
        spread(m, 2, c_own, d_zm).start()
        attn[m] = attended(r + 1 - xi, sub)
        hand_over(m).start()
        spread_sibling(m, 0)

    def turn1(m):
        spread(m, 0, c_x).wait_recv()
        spread(m, 3, c_x, d_zp).start()
        spread(m, 4, c_x, d_zm).start()
        spread_sibling(m, 1)
        spread(m, 1, c_m).wait_recv()
        spread(m, 5, c_m, d_zp).start()
        spread_sibling(m, 2)
        spread(m, 2, c_p).wait_recv()
        spread_sibling(m, 3)

    def turn2(m):
        spread(m, 4, c_xp).wait_recv()
        spread(m, 6, c_xp, d_zm).start()
        spread_sibling(m, 5)
        spread(m, 3, c_xm).wait_recv()
        spread_sibling(m, 4)

    def turn3(m):
        spread(m, 5, c_2).wait_recv()
        spread_sibling(m, 6)
        spread(m, 6, c_x2).wait_recv()
        spread_sibling(m, 7)

    def out_rows(m):
        return pl.ds(pl.multiple_of((2 * div(m, 2) + xi) * BLOCK + rem(m, 2) * OC, OC), OC)

    def out_chunk(m):
        return 2 * (2 * div(m, 2) + xi) + rem(m, 2)

    def result(m, n):
        return remote(outb.at[m, n], out.at[out_rows(m)], r_s.at[m, n], r_r.at[out_chunk(m)],
                      at(y, half, 2 * c + n, z))

    def result_local(m, n):
        return pltpu.make_async_copy(outb.at[m, n], out.at[out_rows(m)], r_r.at[out_chunk(m)])

    def turn4(m):
        for piece in range(8):
            spread(m, SIB3 + piece, sib_cols[piece]).wait_recv()

        def multiply(n, _):
            outb[m, n] = jnp.dot(ag[m], wog[n], preferred_element_type=F32).astype(BF)
            here = jnp.logical_and(mine, n == xi)

            @pl.when(here)
            def _():
                result_local(m, n).start()

            @pl.when(jnp.logical_not(here))
            def _():
                result(m, n).start()
            return 0
        lax.fori_loop(0, 2, multiply, 0)

    def round3(k, _):
        @pl.when(k < NO)
        def _():
            turn0(k)

        @pl.when(jnp.logical_and(k >= 1, k < NO + 1))
        def _():
            turn1(k - 1)

        @pl.when(jnp.logical_and(k >= 2, k < NO + 2))
        def _():
            turn2(k - 2)

        @pl.when(jnp.logical_and(k >= 3, k < NO + 3))
        def _():
            turn3(k - 3)

        @pl.when(k == 4)
        def _():
            for d in (1, 2, 3):
                o_third(d).wait_recv()

        @pl.when(k >= 4)
        def _():
            turn4(k - 4)
        return 0
    lax.fori_loop(0, NO + 4, round3, 0)

    g_rows = [XF] * 7 + [ZF] * 3 + [Z1, Z2] + [ZF] * 3 + [ALL] * 8

    def sent1(r, _):
        for k, rows in enumerate(g_rows):
            gather(r, k, rows, c_own).wait_send()
        return 0
    lax.fori_loop(0, NB, sent1, 0)

    def sent3(m, _):
        for k in range(15):
            spread(m, k, c_own).wait_send()
        for n in range(2):
            @pl.when(jnp.logical_not(jnp.logical_and(mine, n == xi)))
            def _(n=n):
                result(m, n).wait_send()
        return 0
    lax.fori_loop(0, NO, sent3, 0)

    @pl.when(other)
    def _():
        for r in range(NB):
            tok_remote(r).wait_send()
        for n in range(3):
            w_first(n).wait_send()
            for d in (1, 2, 3):
                w_second(n, d).wait_send()
    for d in (1, 2, 3):
        o_first(d).wait_send()
        o_second(d).wait_send()
        o_third(d).wait_send()

    def sent_state(to, _):
        state_copy(to).wait_send()
        return 0
    lax.fori_loop(shard + 1, 8, sent_state, 0)

    def landed(k, _):
        rows = pl.ds(pl.multiple_of(k * OC, OC), OC)
        pltpu.make_async_copy(outb.at[0, 0], out.at[rows], r_r.at[k]).wait()
        return 0
    lax.fori_loop(0, 16, landed, 0)


def local(scale, tokens, w_query, w_key, w_value, w_output):
    rows, feat = tokens.shape
    wide = w_query.shape[0]
    dma, vmem = pltpu.SemaphoreType.DMA, pltpu.VMEM
    return pl.pallas_call(
        lambda *refs: kernel(scale, *refs),
        out_shape=jax.ShapeDtypeStruct((rows, feat), BF),
        in_specs=[pl.BlockSpec(memory_space=pl.ANY)] * 5,
        out_specs=pl.BlockSpec(memory_space=pl.ANY),
        scratch_shapes=[
            vmem((NB, BLOCK, wide), BF),
            vmem((3, wide, FEAT), BF),
            vmem((NB, BLOCK, FEAT), BF),
            vmem((3, BLOCK, FEAT), BF),
            vmem((NB, BLOCK, FEAT), F32),
            vmem((NB, 2, DH, DH), F32),
            vmem((2, DH, DH), F32),
            vmem((2, DH, DH), BF),
            vmem((8, 2, DH, DH), BF),
            vmem((NB, 2, DH, DH), BF),
            vmem((NO, OC, FEAT), BF),
            vmem((NO, OC, wide), BF),
            vmem((2, wide, FEAT), BF),
            vmem((NO, 2, OC, FEAT), BF),
            dma((NB,)), dma((NB,)),
            dma((3,)),
            dma((3,)), dma((3,)),
            dma((3, 4)), dma((3, 4)),
            dma((4,)), dma((4,)),
            dma((4,)), dma((4,)),
            dma((4,)), dma((4,)),
            dma((NB, 23)), dma((NB, 23)),
            dma((8,)), dma((8,)),
            dma((NO, 15)), dma((NO, 15)),
            dma((NO, 2)), dma((16,)),
        ],
        name="layer",
        cost_estimate=pl.CostEstimate(flops=18_000_000_000, bytes_accessed=12 << 20, transcendentals=0),
        compiler_params=pltpu.CompilerParams(
            collective_id=0, has_side_effects=True, vmem_limit_bytes=56 << 20),
    )(tokens, w_query, w_key, w_value, w_output)


def solution(mesh):
    scale = 1.0 / math.sqrt(DH * 16384)
    in_specs = (
        P("seq", "tensor"),
        P(None, "tensor"),
        P(None, "tensor"),
        P(None, "tensor"),
        P("tensor", None),
    )
    return jax.shard_map(
        lambda *args: local(scale, *args),
        mesh=mesh, in_specs=in_specs, out_specs=P("seq", "tensor"), check_vma=False)
```

```python
import math

import jax
import jax.numpy as jnp
from jax import lax
from jax.experimental import pallas as pl
from jax.experimental.pallas import tpu as pltpu
from jax.sharding import PartitionSpec as P

DH = 128
BLOCK = 256
BF = jnp.bfloat16
F32 = jnp.float32
NB = 8
CH = 128
NC = 16
RX = 80
RZ = CH - RX
HZ = 32
OC = 128
NO = 8
FEAT = 256
SIB = 15
SIB3 = 7
AHEAD = 1
LATE = 12
AHEAD3 = 1


def remote(src, dst, send, recv, device):
    return pltpu.make_async_remote_copy(
        src_ref=src, dst_ref=dst, send_sem=send, recv_sem=recv,
        device_id=device, device_id_type=pl.DeviceIdType.MESH,
    )


def wide_rows(gathered, index):
    return jnp.concatenate([gathered[index, p] for p in range(16)], axis=1)


def kernel(scale, tok, wq, wk, wv, wo, out,
           xg, w, q, qkv, intra, st, run, tot, carry, low, attn, ag, wog, outb,
           pre_s, pre_r, w_l, w1_s, w1_r, w2_s, w2_r, o1_s, o1_r, o2_s, o2_r, o3_s, o3_r,
           g_s, g_r, t_s, t_r, a_s, a_r, r_s, r_r):
    div, rem = lax.div, lax.rem
    seq, ten = lax.axis_index("seq"), lax.axis_index("tensor")
    y, c, x, z = div(seq, 2), rem(seq, 2), div(ten, 4), rem(ten, 4)
    half, xi = div(x, 2), rem(x, 2)
    xn, xc = x + 1 - 2 * xi, 3 - x
    xd = 3 - xn
    mine = c == half
    other = jnp.logical_not(mine)
    shard = 2 * y + half
    zp, zm, z2 = rem(z + 1, 4), rem(z + 3, 4), rem(z + 2, 4)

    def at(y_, c_, x_, z_):
        return (2 * y_ + c_, 4 * x_ + z_)

    d_xn, d_zp, d_zm = at(y, c, xn, z), at(y, c, x, zp), at(y, c, x, zm)
    d_sib, d_part = at(y, 1 - c, x, z), at(y, 1 - c, xc, z)

    def col(x_, z_):
        return jnp.where(mine, x_, 3 - x_) * 4 + z_

    places = ((x, z), (xn, z), (x, zm), (x, zp), (xn, zm), (xn, zp), (x, z2), (xn, z2))
    cols = [col(*p) for p in places]
    c_own, c_x, c_m, c_p, c_xm, c_xp, c_2, c_x2 = cols

    barrier = pltpu.get_barrier_semaphore()
    peers = [d_sib, d_part, at(y, 1 - c, xd, z)]
    for d in (1, 2, 3):
        peers += [at(y, c, x, rem(z + d, 4)), at(y, c, rem(x + d, 4), z),
                  at(rem(y + d, 4), c, x, z), at(rem(y + d, 4), c, xc, z)]
    for peer in peers:
        pl.semaphore_signal(barrier, inc=1, device_id=peer, device_id_type=pl.DeviceIdType.MESH)
    pl.semaphore_wait(barrier, len(peers))

    w_hbm = (wq, wk, wv)
    quarter = pl.ds(pl.multiple_of(y * 1024, 1024), 1024)

    def tok_rows(r):
        return tok.at[pl.ds(pl.multiple_of(r * CH, CH), CH)]

    def slot(r, piece, first=0, count=CH):
        rows = pl.ds(pl.multiple_of(rem(r, 2) * CH + first, 16), count)
        return xg.at[div(r, 2), piece, rows]

    def tok_local(r):
        return pltpu.make_async_copy(tok_rows(r), slot(r, ten), pre_r.at[r])

    def tok_remote(r):
        return remote(tok_rows(r), slot(r, ten), pre_s.at[r], pre_r.at[r], d_part)

    def tok_wait(r):
        pltpu.make_async_copy(tok_rows(r), slot(r, c_own), pre_r.at[r]).wait()

    def w_local(n):
        return pltpu.make_async_copy(w_hbm[n], w.at[n], w_l.at[n])

    def w_first(n):
        return remote(w_hbm[n].at[quarter], w.at[n, quarter], w1_s.at[n], w1_r.at[n], d_part)

    yp, ym, y2 = rem(y + 1, 4), rem(y + 3, 4), rem(y + 2, 4)
    d_yp, d_ym = at(yp, c, x, z), at(ym, c, x, z)

    def w_copy(n, k, y_, first, count, device=None):
        rows = pl.ds(pl.multiple_of(y_ * 1024 + first, 16), count)
        return remote(w.at[n, rows], w.at[n, rows], w2_s.at[n, k], w2_r.at[n, k], d_yp if device is None else device)

    def w_second(n):
        return [w_copy(n, 0, y, 0, 1024, d_yp), w_copy(n, 1, y, 0, 1024, d_ym)]

    def w_second_in(n):
        return [w_copy(n, 0, ym, 0, 1024), w_copy(n, 1, yp, 0, 1024)]

    def w_third(n):
        return [w_copy(n, 2, ym, 0, 512, d_yp), w_copy(n, 3, yp, 512, 512, d_ym)]

    def w_third_in(n):
        return [w_copy(n, 2, y2, 0, 512), w_copy(n, 3, y2, 512, 512)]

    o_cols = pl.ds(pl.multiple_of(rem(y, 2) * DH, DH), DH)
    o_blk = div(y, 2)

    def o_source(z_):
        return wo.at[:, pl.ds(pl.multiple_of(((2 * c + o_blk) * 4 + z_) * FEAT + rem(y, 2) * DH, DH), DH)]

    o_mine = wog.at[o_blk, pl.ds(pl.multiple_of(ten * FEAT, FEAT), FEAT), o_cols]

    def o_first(d):
        if d == 0:
            return pltpu.make_async_copy(o_source(z), o_mine, o1_r.at[0])
        to = rem(z + d, 4)
        return remote(o_source(to), o_mine, o1_s.at[d], o1_r.at[d], at(y, c, x, to))

    def o_part(k, x_, to, first=0, count=1024):
        rows = pl.ds(pl.multiple_of(x_ * 1024 + first, 16), count)
        part = wog.at[o_blk, rows, o_cols]
        place = div(first, 128) if k == 0 and count < 1024 else 8
        return remote(part, part, o2_s.at[k], o2_r.at[k, place], at(y, c, to, z))

    def o_copy(k, y_, first, count, device=None):
        rows, columns = pl.ds(pl.multiple_of(first, 16), count), pl.ds(pl.multiple_of(rem(y_, 2) * DH, DH), DH)
        part = wog.at[div(y_, 2), rows, columns]
        return remote(part, part, o3_s.at[k], o3_r.at[k], d_yp if device is None else device)

    def o_third(x_):
        return [o_copy(0, y, x_ * 1024, 1024, d_yp), o_copy(1, y, x_ * 1024, 1024, d_ym)]

    def o_third_out():
        return [o_copy(0, y, 0, 4096, d_yp), o_copy(1, y, 0, 4096, d_ym)]

    def o_third_in():
        return [o_copy(0, ym, 0, 4096), o_copy(1, yp, 0, 4096)]

    def o_fourth():
        return [o_copy(2, ym, 0, 2048, d_yp), o_copy(3, yp, 2048, 2048, d_ym)]

    def o_fourth_in():
        return [o_copy(2, y2, 0, 2048), o_copy(3, y2, 2048, 2048)]

    @pl.when(mine)
    def _():
        def start(r, _):
            tok_local(r).start()
            return 0
        lax.fori_loop(0, NC, start, 0)
        for n in range(3):
            w_local(n).start()

    def send_inputs(k):
        for step in range(4):
            @pl.when(jnp.logical_and(other, k == 2 * step))
            def _(step=step):
                for r in range(4 * step, 4 * step + 4):
                    tok_remote(r).start()
                if step < 3:
                    w_first(step).start()
        for step in range(3):
            @pl.when(jnp.logical_and(other, k == 2 * step + 3))
            def _(step=step):
                w_first(step).wait_recv()
                for copy in w_second(step):
                    copy.start()

            @pl.when(jnp.logical_and(other, k == 2 * step + 5))
            def _(step=step):
                for copy, forward in zip(w_second_in(step), w_third(step)):
                    copy.wait_recv()
                    forward.start()

        @pl.when(k == 0)
        def _():
            for d in range(4):
                o_first(d).start()

        @pl.when(k == 2)
        def _():
            o_first(0).wait()
            for d in (1, 2, 3):
                o_first(d).wait_recv()

        @pl.when(jnp.logical_and(k >= 2, k < 10))
        def _():
            o_part(0, x, xn, (k - 2) * 128, 128).start()
            o_part(1, x, xc, (k - 2) * 128, 128).start()

        @pl.when(jnp.logical_and(k >= 4, k < 12))
        def _():
            o_part(0, xn, xn, (k - 4) * 128, 128).wait_recv()
            o_part(2, xn, xc, (k - 4) * 128, 128).start()

        def third(x_):
            for copy in o_third(x_):
                copy.start()

        @pl.when(k == 8)
        def _():
            third(x)

        @pl.when(k == 12)
        def _():
            third(xn)
            o_part(1, xc, xn).wait_recv()
            third(xc)

        @pl.when(k == 14)
        def _():
            o_part(2, xd, xn).wait_recv()
            third(xd)

    ALL, XF, ZF, Z1, Z2 = (0, CH), (0, RX), (RX, RZ), (RX, HZ), (RX + HZ, RZ - HZ)

    def gather(r, k, rows, column, device=None):
        part = slot(r, column, *rows)
        return remote(part, part, g_s.at[r], g_r.at[r, k], d_sib if device is None else device)

    def to_sibling(r, piece):
        gather(r, SIB, ALL, cols[piece]).start()

    c_long, c_short = jnp.where(c == 0, c_m, c_p), jnp.where(c == 0, c_p, c_m)
    d_long, d_short = at(y, c, x, jnp.where(c == 0, zp, zm)), at(y, c, x, jnp.where(c == 0, zm, zp))

    def hop0(r):
        tok_wait(r)
        gather(r, 0, XF, c_own, d_xn).start()
        gather(r, 8, ZF, c_own, d_zp).start()
        gather(r, 9, ZF, c_own, d_zm).start()
        gather(r, 1, XF, c_own, d_zp).start()
        gather(r, 2, XF, c_own, d_zm).start()
        gather(r, 7, ZF, c_own, d_xn).start()
        to_sibling(r, 0)

    def hop1(r):
        gather(r, 0, XF, c_x).wait_recv()
        gather(r, 3, XF, c_x, d_zp).start()
        gather(r, 4, XF, c_x, d_zm).start()
        gather(r, 8, ZF, c_m).wait_recv()
        gather(r, 12, ZF, c_m, d_xn).start()
        gather(r, 9, ZF, c_p).wait_recv()
        gather(r, 13, ZF, c_p, d_xn).start()
        gather(r, 10, Z1, c_long, d_long).start()
        gather(r, 11, Z2, c_short, d_short).start()
        gather(r, 1, XF, c_m).wait_recv()
        gather(r, 5, XF, c_m, d_zp).start()
        to_sibling(r, 2)
        gather(r, 2, XF, c_p).wait_recv()
        to_sibling(r, 3)
        gather(r, 7, ZF, c_x).wait_recv()
        to_sibling(r, 1)

    def hop2(r):
        gather(r, 4, XF, c_xp).wait_recv()
        gather(r, 6, XF, c_xp, d_zm).start()
        gather(r, 10, Z1, c_2).wait_recv()
        gather(r, 11, Z2, c_2).wait_recv()
        gather(r, 14, ZF, c_2, d_xn).start()
        gather(r, 3, XF, c_xm).wait_recv()
        gather(r, 12, ZF, c_xm).wait_recv()
        to_sibling(r, 4)
        gather(r, 13, ZF, c_xp).wait_recv()
        to_sibling(r, 5)

    def hop3(r):
        gather(r, 5, XF, c_2).wait_recv()
        to_sibling(r, 6)
        gather(r, 6, XF, c_x2).wait_recv()
        gather(r, 14, ZF, c_x2).wait_recv()
        to_sibling(r, 7)

    def heads(n):
        return slice(n * DH, (n + 1) * DH)

    def state_copy(to):
        to_y, to_half = div(to, 2), rem(to, 2)
        to_x = jnp.where(to_half == half, x, xc)
        return remote(tot, carry.at[shard], t_s.at[to], t_r.at[shard], at(to_y, c, to_x, z))

    def project(r, n):
        qkv[n] = jnp.dot(wide_rows(xg, r), w[n], preferred_element_type=F32).astype(BF)

    def step_key(r):
        for half_block in range(2):
            eight = xg.at[r, pl.ds(0, 4)]
            remote(eight, eight, g_s.at[2 * r], g_r.at[2 * r + half_block, SIB], d_sib).wait_recv()
        project(r, 1)

    def step_value(r):
        project(r, 2)
        for n in range(2):
            total = run[n]
            st[r, n] = total
            run[n] = total + lax.dot_general(
                qkv[1, :, heads(n)], qkv[2, :, heads(n)], (((0,), (0,)), ((), ())), preferred_element_type=F32)

        @pl.when(r == NB - 1)
        def _():
            tot[...] = run[...].astype(BF)

            def send(to, _):
                state_copy(to).start()
                return 0
            lax.fori_loop(shard + 1, 8, send, 0)

    def step_query(r):
        project(r, 0)
        q[r] = qkv[0]

    def step_attend(r):
        causal = (lax.broadcasted_iota(jnp.int32, (BLOCK, BLOCK), 0)
                  >= lax.broadcasted_iota(jnp.int32, (BLOCK, BLOCK), 1))
        for n in range(2):
            scores = lax.dot_general(
                qkv[0, :, heads(n)], qkv[1, :, heads(n)], (((1,), (1,)), ((), ())), preferred_element_type=F32)
            scores = jnp.where(causal, scores, 0.0).astype(BF)
            intra[r, :, heads(n)] = jnp.dot(scores, qkv[2, :, heads(n)], preferred_element_type=F32)

    run[...] = jnp.zeros_like(run)

    send_inputs(0)
    for r in range(AHEAD):
        hop0(r)

    def done(k):
        return jnp.maximum(jnp.minimum(jnp.where(mine, NB, k - LATE + 1), div(k - 3, 2)), 0)

    def round1(k, _):
        block = done(k - 1)
        busy = done(k) > block

        @pl.when(k > 0)
        def _():
            send_inputs(k)

        @pl.when(k < NC - AHEAD)
        def _():
            hop0(k + AHEAD)

        @pl.when(jnp.logical_and(mine, k == 5))
        def _():
            for n in range(3):
                w_local(n).wait()

        @pl.when(jnp.logical_and(other, k == LATE))
        def _():
            for n in range(3):
                for copy in w_third_in(n):
                    copy.wait_recv()

        steps = (step_key, step_value, step_query, step_attend)
        for late, (hop, step) in enumerate(zip((None, hop1, hop2, hop3), steps)):
            if hop is not None:
                @pl.when(jnp.logical_and(k >= late, k < NC + late))
                def _(hop=hop, late=late):
                    hop(k - late)

            @pl.when(busy)
            def _(step=step):
                step(block)
        return 0
    lax.fori_loop(0, NC + 4, round1, 0)

    run[...] = jnp.zeros_like(run)

    def add(k, _):
        remote(tot, carry.at[k], t_s.at[k], t_r.at[k], d_sib).wait_recv()
        run[...] += carry[k].astype(F32)
        return 0
    lax.fori_loop(0, shard, add, 0)

    def lower(r, _):
        low[r] = (st[r] + run[...]).astype(BF)
        return 0
    lax.fori_loop(0, NB, lower, 0)

    for copy, forward in zip(o_third_in(), o_fourth()):
        copy.wait_recv()
        forward.start()

    def attended(r, first):
        rows = pl.ds(pl.multiple_of(first, OC), OC)
        parts = []
        for n in range(2):
            inter = jnp.dot(q[r, rows, heads(n)], low[r, n], preferred_element_type=F32)
            parts.append(((inter + intra[r, rows, heads(n)]) * scale).astype(BF))
        return jnp.concatenate(parts, axis=1)

    def slot3(m, piece):
        return ag.at[m, piece]

    def spread(m, k, column, device=None):
        part = slot3(m, column)
        return remote(part, part, a_s.at[m], a_r.at[m, k], d_sib if device is None else device)

    def spread_sibling(m, piece):
        spread(m, SIB3, cols[piece]).start()

    def hand_over(m):
        return remote(attn.at[m], slot3(m, c_own), a_s.at[m], a_r.at[m, 0], d_xn)

    def turn0(m):
        r, first = 2 * div(m, 2), rem(m, 2) * OC
        slot3(m, c_own)[...] = attended(r + xi, first)
        spread(m, 1, c_own, d_zp).start()
        spread(m, 2, c_own, d_zm).start()
        attn[m] = attended(r + 1 - xi, first)
        hand_over(m).start()
        spread_sibling(m, 0)

    def turn1(m):
        spread(m, 0, c_x).wait_recv()
        spread(m, 3, c_x, d_zp).start()
        spread(m, 4, c_x, d_zm).start()
        spread_sibling(m, 1)
        spread(m, 1, c_m).wait_recv()
        spread(m, 5, c_m, d_zp).start()
        spread_sibling(m, 2)
        spread(m, 2, c_p).wait_recv()
        spread_sibling(m, 3)

    def turn2(m):
        spread(m, 4, c_xp).wait_recv()
        spread(m, 6, c_xp, d_zm).start()
        spread_sibling(m, 5)
        spread(m, 3, c_xm).wait_recv()
        spread_sibling(m, 4)

    def turn3(m):
        spread(m, 5, c_2).wait_recv()
        spread_sibling(m, 6)
        spread(m, 6, c_x2).wait_recv()
        spread_sibling(m, 7)

    def out_rows(m):
        return pl.ds(pl.multiple_of((2 * div(m, 2) + xi) * BLOCK + rem(m, 2) * OC, OC), OC)

    def result(m, n):
        return remote(outb.at[m, n], out.at[out_rows(m)], r_s.at[m, n], r_r.at[0],
                      at(y, half, 2 * c + n, z))

    def result_local(m, n):
        return pltpu.make_async_copy(outb.at[m, n], out.at[out_rows(m)], r_r.at[0])

    def turn4(m):
        eight = ag.at[m, pl.ds(0, 8)]
        remote(eight, eight, a_s.at[m], a_r.at[m, SIB3], d_sib).wait_recv()

        def multiply(n, _):
            outb[m, n] = jnp.dot(wide_rows(ag, m), wog[n], preferred_element_type=F32).astype(BF)
            here = jnp.logical_and(mine, n == xi)

            @pl.when(here)
            def _():
                result_local(m, n).start()

            @pl.when(jnp.logical_not(here))
            def _():
                result(m, n).start()
            return 0
        lax.fori_loop(0, 2, multiply, 0)

    for m in range(AHEAD3):
        turn0(m)

    def round3(k, _):
        @pl.when(k < NO - AHEAD3)
        def _():
            turn0(k + AHEAD3)

        @pl.when(jnp.logical_and(k >= 1, k < NO + 1))
        def _():
            turn1(k - 1)

        @pl.when(jnp.logical_and(k >= 2, k < NO + 2))
        def _():
            turn2(k - 2)

        @pl.when(jnp.logical_and(k >= 3, k < NO + 3))
        def _():
            turn3(k - 3)

        @pl.when(k == 4)
        def _():
            for copy in o_fourth_in():
                copy.wait_recv()

        @pl.when(k >= 4)
        def _():
            turn4(k - 4)
        return 0
    lax.fori_loop(0, NO + 4, round3, 0)

    def sent1(r, _):
        part = xg.at[0, pl.ds(0, 15), pl.ds(0, CH)]
        pltpu.make_async_copy(part, part, g_s.at[r]).wait()
        return 0
    lax.fori_loop(0, NC, sent1, 0)

    def sent3(m, _):
        part = ag.at[m, pl.ds(0, 15)]
        pltpu.make_async_copy(part, part, a_s.at[m]).wait()
        return 0
    lax.fori_loop(0, NO, sent3, 0)

    def sent_result(m, _):
        for n in range(2):
            @pl.when(jnp.logical_not(jnp.logical_and(mine, n == xi)))
            def _(n=n):
                result(m, n).wait_send()
        return 0
    lax.fori_loop(0, NO, sent_result, 0)

    @pl.when(other)
    def _():
        for r in range(NC):
            tok_remote(r).wait_send()
        for n in range(3):
            for copy in [w_first(n)] + w_second(n) + w_third(n):
                copy.wait_send()
    for copy in [o_first(d) for d in (1, 2, 3)] + [o_part(k, x, xn) for k in range(3)] + o_third_out() + o_fourth():
        copy.wait_send()

    def sent_state(to, _):
        state_copy(to).wait_send()
        return 0
    lax.fori_loop(shard + 1, 8, sent_state, 0)

    pltpu.make_async_copy(tok, out, r_r.at[0]).wait()


def local(scale, tokens, w_query, w_key, w_value, w_output):
    rows, feat = tokens.shape
    wide = w_query.shape[0]
    dma, vmem = pltpu.SemaphoreType.DMA, pltpu.VMEM
    return pl.pallas_call(
        lambda *refs: kernel(scale, *refs),
        out_shape=jax.ShapeDtypeStruct((rows, feat), BF),
        in_specs=[pl.BlockSpec(memory_space=pl.ANY)] * 5,
        out_specs=pl.BlockSpec(memory_space=pl.ANY),
        scratch_shapes=[
            vmem((NB, 16, BLOCK, FEAT), BF),
            vmem((3, wide, FEAT), BF),
            vmem((NB, BLOCK, FEAT), BF),
            vmem((3, BLOCK, FEAT), BF),
            vmem((NB, BLOCK, FEAT), F32),
            vmem((NB, 2, DH, DH), F32),
            vmem((2, DH, DH), F32),
            vmem((2, DH, DH), BF),
            vmem((8, 2, DH, DH), BF),
            vmem((NB, 2, DH, DH), BF),
            vmem((NO, OC, FEAT), BF),
            vmem((NO, 16, OC, FEAT), BF),
            vmem((2, wide, FEAT), BF),
            vmem((NO, 2, OC, FEAT), BF),
            dma((NC,)), dma((NC,)),
            dma((3,)),
            dma((3,)), dma((3,)),
            dma((3, 4)), dma((3, 4)),
            dma((4,)), dma((4,)),
            dma((3,)), dma((3, 9)),
            dma((4,)), dma((4,)),
            dma((NC,)), dma((NC, 16)),
            dma((8,)), dma((8,)),
            dma((NO,)), dma((NO, 8)),
            dma((NO, 2)), dma((1,)),
        ],
        name="layer",
        cost_estimate=pl.CostEstimate(flops=18_000_000_000, bytes_accessed=12 << 20, transcendentals=0),
        compiler_params=pltpu.CompilerParams(
            collective_id=0, has_side_effects=True, vmem_limit_bytes=56 << 20),
    )(tokens, w_query, w_key, w_value, w_output)


def solution(mesh):
    scale = 1.0 / math.sqrt(DH * 16384)
    in_specs = (
        P("seq", "tensor"),
        P(None, "tensor"),
        P(None, "tensor"),
        P(None, "tensor"),
        P("tensor", None),
    )
    return jax.shard_map(
        lambda *args: local(scale, *args),
        mesh=mesh, in_specs=in_specs, out_specs=P("seq", "tensor"), check_vma=False)
```

```python
import math

import jax
import jax.numpy as jnp
from jax import lax
from jax.experimental import pallas as pl
from jax.experimental.pallas import tpu as pltpu
from jax.sharding import PartitionSpec as P

DH = 128
BLOCK = 256
BF = jnp.bfloat16
F32 = jnp.float32
NB = 8
CH = 128
NC = 16
RX = 80
RZ = CH - RX
HZ = 32
OC = 128
NO = 8
FEAT = 256
SIB = 15
SIB3 = 7
AHEAD = 1
WP = 128
FULL = 6
OP = 64
THIRD = 12
LATE = 12
AHEAD3 = 1


def remote(src, dst, send, recv, device):
    return pltpu.make_async_remote_copy(
        src_ref=src, dst_ref=dst, send_sem=send, recv_sem=recv,
        device_id=device, device_id_type=pl.DeviceIdType.MESH,
    )


def wide_rows(gathered, index):
    return jnp.concatenate([gathered[index, p] for p in range(16)], axis=1)


def kernel(scale, tok, wq, wk, wv, wo, out,
           xg, w, q, qkv, intra, st, run, tot, carry, low, attn, ag, wog, outb,
           pre_s, pre_r, w_l, w1_s, w1_r, w2_s, w2_r, w3_s, w3_r, o1_s, o1_r, o2_s, o2_r, o3_s, o3_r,
           g_s, g_r, t_s, t_r, a_s, a_r, r_s, r_r):
    div, rem = lax.div, lax.rem
    seq, ten = lax.axis_index("seq"), lax.axis_index("tensor")
    y, c, x, z = div(seq, 2), rem(seq, 2), div(ten, 4), rem(ten, 4)
    half, xi = div(x, 2), rem(x, 2)
    xn, xc = x + 1 - 2 * xi, 3 - x
    xd = 3 - xn
    mine = c == half
    other = jnp.logical_not(mine)
    shard = 2 * y + half
    zp, zm, z2 = rem(z + 1, 4), rem(z + 3, 4), rem(z + 2, 4)

    def at(y_, c_, x_, z_):
        return (2 * y_ + c_, 4 * x_ + z_)

    d_xn, d_zp, d_zm = at(y, c, xn, z), at(y, c, x, zp), at(y, c, x, zm)
    d_sib, d_part = at(y, 1 - c, x, z), at(y, 1 - c, xc, z)

    def col(x_, z_):
        return jnp.where(mine, x_, 3 - x_) * 4 + z_

    places = ((x, z), (xn, z), (x, zm), (x, zp), (xn, zm), (xn, zp), (x, z2), (xn, z2))
    cols = [col(*p) for p in places]
    c_own, c_x, c_m, c_p, c_xm, c_xp, c_2, c_x2 = cols

    barrier = pltpu.get_barrier_semaphore()
    peers = [d_sib, d_part, at(y, 1 - c, xd, z)]
    for d in (1, 2, 3):
        peers += [at(y, c, x, rem(z + d, 4)), at(y, c, rem(x + d, 4), z),
                  at(rem(y + d, 4), c, x, z), at(rem(y + d, 4), c, xc, z)]
    for peer in peers:
        pl.semaphore_signal(barrier, inc=1, device_id=peer, device_id_type=pl.DeviceIdType.MESH)
    pl.semaphore_wait(barrier, len(peers))

    w_hbm = (wq, wk, wv)
    quarter = pl.ds(pl.multiple_of(y * 1024, 1024), 1024)

    def tok_rows(r):
        return tok.at[pl.ds(pl.multiple_of(r * CH, CH), CH)]

    def slot(r, piece, first=0, count=CH):
        rows = pl.ds(pl.multiple_of(rem(r, 2) * CH + first, 16), count)
        return xg.at[div(r, 2), piece, rows]

    def tok_local(r):
        return pltpu.make_async_copy(tok_rows(r), slot(r, ten), pre_r.at[r])

    def tok_remote(r):
        return remote(tok_rows(r), slot(r, ten), pre_s.at[r], pre_r.at[r], d_part)

    def tok_wait(r):
        pltpu.make_async_copy(tok_rows(r), slot(r, c_own), pre_r.at[r]).wait()

    def w_local(n):
        return pltpu.make_async_copy(w_hbm[n], w.at[n], w_l.at[n])

    def w_rows(y_, i, first=0, count=WP):
        return pl.ds(pl.multiple_of(y_ * 1024 + i * WP + first, 16), count)

    def w_first(n, i):
        rows = w_rows(y, i)
        return remote(w_hbm[n].at[rows], w.at[n, rows], w1_s.at[0], w1_r.at[i], at(y, c, xc, z))

    yp, ym, y2 = rem(y + 1, 4), rem(y + 3, 4), rem(y + 2, 4)
    d_yp, d_ym = at(yp, c, x, z), at(ym, c, x, z)

    def w_second(n, i):
        part = w.at[n, w_rows(y, i)]
        return [remote(part, part, w2_s.at[k], w2_r.at[k, i], to) for k, to in enumerate((d_yp, d_ym))]

    def w_third(n, i):
        parts = w.at[n, w_rows(ym, i, 0, WP // 2)], w.at[n, w_rows(yp, i, WP // 2, WP // 2)]
        return [remote(part, part, w3_s.at[k], w3_r.at[k], to) for k, (part, to) in enumerate(zip(parts, (d_yp, d_ym)))]

    def w_wait(rows, semaphore):
        part = w.at[:, pl.ds(0, rows)]
        pltpu.make_async_copy(part, part, semaphore).wait()

    o_cols = pl.ds(pl.multiple_of(rem(y, 2) * DH, DH), DH)
    o_blk = div(y, 2)

    def o_source(z_):
        return wo.at[:, pl.ds(pl.multiple_of(((2 * c + o_blk) * 4 + z_) * FEAT + rem(y, 2) * DH, DH), DH)]

    o_mine = wog.at[o_blk, pl.ds(pl.multiple_of(ten * FEAT, FEAT), FEAT), o_cols]

    def o_first(d):
        if d == 0:
            return pltpu.make_async_copy(o_source(z), o_mine, o1_r.at[0])
        to = rem(z + d, 4)
        return remote(o_source(to), o_mine, o1_s.at[d], o1_r.at[d], at(y, c, x, to))

    def o_part(k, x_, to, i, count=OP):
        rows = pl.ds(pl.multiple_of(x_ * 1024 + i * OP, OP), count)
        part = wog.at[o_blk, rows, o_cols]
        return remote(part, part, o2_s.at[k], o2_r.at[k, i], at(y, c, to, z))

    def o_copy(k, y_, first, count, device=None):
        rows, columns = pl.ds(pl.multiple_of(first, 16), count), pl.ds(pl.multiple_of(rem(y_, 2) * DH, DH), DH)
        part = wog.at[div(y_, 2), rows, columns]
        return remote(part, part, o3_s.at[k], o3_r.at[k], d_yp if device is None else device)

    def o_third(x_, i):
        first = x_ * 1024 + i * WP
        return [o_copy(0, y, first, WP, d_yp), o_copy(1, y, first, WP, d_ym)]

    def o_third_out():
        return [o_copy(0, y, 0, 4096, d_yp), o_copy(1, y, 0, 4096, d_ym)]

    def o_third_in():
        return [o_copy(0, ym, 0, 4096), o_copy(1, yp, 0, 4096)]

    def o_fourth(i):
        return [o_copy(2, ym, i * WP, WP, d_yp), o_copy(3, yp, 2048 + i * WP, WP, d_ym)]

    def o_fourth_out():
        return [o_copy(2, ym, 0, 2048), o_copy(3, yp, 2048, 2048)]

    def o_fourth_in():
        return [o_copy(2, y2, 0, 2048), o_copy(3, y2, 2048, 2048)]

    @pl.when(mine)
    def _():
        def start(r, _):
            tok_local(r).start()
            return 0
        lax.fori_loop(0, NC, start, 0)
        for n in (1, 2, 0):
            w_local(n).start()

    def send_inputs(k):
        for step in range(4):
            @pl.when(jnp.logical_and(other, k == 2 * step))
            def _(step=step):
                for r in range(4 * step, 4 * step + 4):
                    tok_remote(r).start()
        @pl.when(jnp.logical_and(mine, k < 8))
        def _():
            for n in (1, 2, 0):
                w_first(n, k).start()

        @pl.when(jnp.logical_and(other, jnp.logical_and(k >= 2, k < 10)))
        def _():
            w_wait(WP, w1_r.at[k - 2])
            for n in (1, 2, 0):
                for copy in w_second(n, k - 2):
                    copy.start()

        @pl.when(jnp.logical_and(other, jnp.logical_and(k >= 4, k < 12)))
        def _():
            for d in range(2):
                w_wait(WP, w2_r.at[d, k - 4])
            for n in (1, 2, 0):
                for copy in w_third(n, k - 4):
                    copy.start()

        @pl.when(k == 0)
        def _():
            for d in range(4):
                o_first(d).start()

        @pl.when(k == 2)
        def _():
            o_first(0).wait()
            for d in (1, 2, 3):
                o_first(d).wait_recv()

        def third(x_, i):
            for copy in o_third(x_, i):
                copy.start()

        @pl.when(jnp.logical_and(k >= 2, k < 18))
        def _():
            o_part(0, x, xn, k - 2).start()
            o_part(1, x, xc, k - 2).start()

        @pl.when(jnp.logical_and(k >= 4, k < 20))
        def _():
            o_part(0, xn, xn, k - 4).wait_recv()
            o_part(2, xn, xc, k - 4).start()

        @pl.when(k >= THIRD)
        def _():
            i = k - THIRD
            third(x, i)
            third(xn, i)
            for half_piece in range(2):
                o_part(1, xc, xn, 2 * i + half_piece).wait_recv()
            third(xc, i)

        @pl.when(k >= THIRD + 1)
        def _():
            third_last(k - THIRD - 1)

    def third(x_, i):
        for copy in o_third(x_, i):
            copy.start()

    def third_last(i):
        for half_piece in range(2):
            o_part(2, xd, xn, 2 * i + half_piece).wait_recv()
        third(xd, i)

    ALL, XF, ZF, Z1, Z2 = (0, CH), (0, RX), (RX, RZ), (RX, HZ), (RX + HZ, RZ - HZ)

    def gather(r, k, rows, column, device=None):
        part = slot(r, column, *rows)
        return remote(part, part, g_s.at[r], g_r.at[r, k], d_sib if device is None else device)

    def to_sibling(r, piece):
        gather(r, SIB, ALL, cols[piece]).start()

    c_long, c_short = jnp.where(c == 0, c_m, c_p), jnp.where(c == 0, c_p, c_m)
    d_long, d_short = at(y, c, x, jnp.where(c == 0, zp, zm)), at(y, c, x, jnp.where(c == 0, zm, zp))

    def hop0(r):
        tok_wait(r)
        gather(r, 0, XF, c_own, d_xn).start()
        gather(r, 8, ZF, c_own, d_zp).start()
        gather(r, 9, ZF, c_own, d_zm).start()
        gather(r, 1, XF, c_own, d_zp).start()
        gather(r, 2, XF, c_own, d_zm).start()
        gather(r, 7, ZF, c_own, d_xn).start()
        to_sibling(r, 0)

    def hop1(r):
        gather(r, 0, XF, c_x).wait_recv()
        gather(r, 3, XF, c_x, d_zp).start()
        gather(r, 4, XF, c_x, d_zm).start()
        gather(r, 8, ZF, c_m).wait_recv()
        gather(r, 12, ZF, c_m, d_xn).start()
        gather(r, 9, ZF, c_p).wait_recv()
        gather(r, 13, ZF, c_p, d_xn).start()
        gather(r, 10, Z1, c_long, d_long).start()
        gather(r, 11, Z2, c_short, d_short).start()
        gather(r, 1, XF, c_m).wait_recv()
        gather(r, 5, XF, c_m, d_zp).start()
        to_sibling(r, 2)
        gather(r, 2, XF, c_p).wait_recv()
        to_sibling(r, 3)
        gather(r, 7, ZF, c_x).wait_recv()
        to_sibling(r, 1)

    def hop2(r):
        gather(r, 4, XF, c_xp).wait_recv()
        gather(r, 6, XF, c_xp, d_zm).start()
        gather(r, 10, Z1, c_2).wait_recv()
        gather(r, 11, Z2, c_2).wait_recv()
        gather(r, 14, ZF, c_2, d_xn).start()
        gather(r, 3, XF, c_xm).wait_recv()
        gather(r, 12, ZF, c_xm).wait_recv()
        to_sibling(r, 4)
        gather(r, 13, ZF, c_xp).wait_recv()
        to_sibling(r, 5)

    def hop3(r):
        gather(r, 5, XF, c_2).wait_recv()
        to_sibling(r, 6)
        gather(r, 6, XF, c_x2).wait_recv()
        gather(r, 14, ZF, c_x2).wait_recv()
        to_sibling(r, 7)

    def heads(n):
        return slice(n * DH, (n + 1) * DH)

    def state_copy(to):
        to_y, to_half = div(to, 2), rem(to, 2)
        to_x = jnp.where(to_half == half, x, xc)
        return remote(tot, carry.at[shard], t_s.at[to], t_r.at[shard], at(to_y, c, to_x, z))

    def project(r, n):
        qkv[n] = jnp.dot(wide_rows(xg, r), w[n], preferred_element_type=F32).astype(BF)

    def step_key(r):
        for half_block in range(2):
            eight = xg.at[r, pl.ds(0, 4)]
            remote(eight, eight, g_s.at[2 * r], g_r.at[2 * r + half_block, SIB], d_sib).wait_recv()
        project(r, 1)

    def step_value(r):
        project(r, 2)
        for n in range(2):
            total = run[n]
            st[r, n] = total
            run[n] = total + lax.dot_general(
                qkv[1, :, heads(n)], qkv[2, :, heads(n)], (((0,), (0,)), ((), ())), preferred_element_type=F32)

        @pl.when(r == NB - 1)
        def _():
            tot[...] = run[...].astype(BF)

            def send(to, _):
                state_copy(to).start()
                return 0
            lax.fori_loop(shard + 1, 8, send, 0)

    def step_query(r):
        project(r, 0)
        q[r] = qkv[0]

    def step_attend(r):
        causal = (lax.broadcasted_iota(jnp.int32, (BLOCK, BLOCK), 0)
                  >= lax.broadcasted_iota(jnp.int32, (BLOCK, BLOCK), 1))
        for n in range(2):
            scores = lax.dot_general(
                qkv[0, :, heads(n)], qkv[1, :, heads(n)], (((1,), (1,)), ((), ())), preferred_element_type=F32)
            scores = jnp.where(causal, scores, 0.0).astype(BF)
            intra[r, :, heads(n)] = jnp.dot(scores, qkv[2, :, heads(n)], preferred_element_type=F32)

    run[...] = jnp.zeros_like(run)

    send_inputs(0)
    for r in range(AHEAD):
        hop0(r)

    def done(k):
        return jnp.maximum(jnp.minimum(jnp.where(mine, NB, k - LATE + 1), div(k - 3, 2)), 0)

    def round1(k, _):
        block = done(k - 1)
        busy = done(k) > block

        @pl.when(k > 0)
        def _():
            send_inputs(k)

        @pl.when(k < NC - AHEAD)
        def _():
            hop0(k + AHEAD)

        @pl.when(jnp.logical_and(mine, k == 5))
        def _():
            for n in range(3):
                w_local(n).wait()

        @pl.when(jnp.logical_and(other, k == LATE))
        def _():
            for d in range(2):
                w_wait(512, w3_r.at[d])

        steps = (step_key, step_value, step_query, step_attend)
        for late, (hop, step) in enumerate(zip((None, hop1, hop2, hop3), steps)):
            if hop is not None:
                @pl.when(jnp.logical_and(k >= late, k < NC + late))
                def _(hop=hop, late=late):
                    hop(k - late)

            @pl.when(busy)
            def _(step=step):
                step(block)
        return 0
    lax.fori_loop(0, NC + 4, round1, 0)

    third_last(7)

    run[...] = jnp.zeros_like(run)

    def add(k, _):
        remote(tot, carry.at[k], t_s.at[k], t_r.at[k], d_sib).wait_recv()
        run[...] += carry[k].astype(F32)
        return 0
    lax.fori_loop(0, shard, add, 0)

    def lower(r, _):
        low[r] = (st[r] + run[...]).astype(BF)
        return 0
    lax.fori_loop(0, NB, lower, 0)

    def attended(r, first):
        rows = pl.ds(pl.multiple_of(first, OC), OC)
        parts = []
        for n in range(2):
            inter = jnp.dot(q[r, rows, heads(n)], low[r, n], preferred_element_type=F32)
            parts.append(((inter + intra[r, rows, heads(n)]) * scale).astype(BF))
        return jnp.concatenate(parts, axis=1)

    def slot3(m, piece):
        return ag.at[m, piece]

    def spread(m, k, column, device=None):
        part = slot3(m, column)
        return remote(part, part, a_s.at[m], a_r.at[m, k], d_sib if device is None else device)

    def spread_sibling(m, piece):
        spread(m, SIB3, cols[piece]).start()

    def hand_over(m):
        return remote(attn.at[m], slot3(m, c_own), a_s.at[m], a_r.at[m, 0], d_xn)

    def turn0(m):
        r, first = 2 * div(m, 2), rem(m, 2) * OC
        slot3(m, c_own)[...] = attended(r + xi, first)
        spread(m, 1, c_own, d_zp).start()
        spread(m, 2, c_own, d_zm).start()
        attn[m] = attended(r + 1 - xi, first)
        hand_over(m).start()
        spread_sibling(m, 0)

    def turn1(m):
        spread(m, 0, c_x).wait_recv()
        spread(m, 3, c_x, d_zp).start()
        spread(m, 4, c_x, d_zm).start()
        spread_sibling(m, 1)
        spread(m, 1, c_m).wait_recv()
        spread(m, 5, c_m, d_zp).start()
        spread_sibling(m, 2)
        spread(m, 2, c_p).wait_recv()
        spread_sibling(m, 3)

    def turn2(m):
        spread(m, 4, c_xp).wait_recv()
        spread(m, 6, c_xp, d_zm).start()
        spread_sibling(m, 5)
        spread(m, 3, c_xm).wait_recv()
        spread_sibling(m, 4)

    def turn3(m):
        spread(m, 5, c_2).wait_recv()
        spread_sibling(m, 6)
        spread(m, 6, c_x2).wait_recv()
        spread_sibling(m, 7)

    def out_rows(m):
        return pl.ds(pl.multiple_of((2 * div(m, 2) + xi) * BLOCK + rem(m, 2) * OC, OC), OC)

    def result(m, n):
        return remote(outb.at[m, n], out.at[out_rows(m)], r_s.at[m, n], r_r.at[0],
                      at(y, half, 2 * c + n, z))

    def result_local(m, n):
        return pltpu.make_async_copy(outb.at[m, n], out.at[out_rows(m)], r_r.at[0])

    def turn4(m):
        eight = ag.at[m, pl.ds(0, 8)]
        remote(eight, eight, a_s.at[m], a_r.at[m, SIB3], d_sib).wait_recv()

        def multiply(n, _):
            outb[m, n] = jnp.dot(wide_rows(ag, m), wog[n], preferred_element_type=F32).astype(BF)
            here = jnp.logical_and(mine, n == xi)

            @pl.when(here)
            def _():
                result_local(m, n).start()

            @pl.when(jnp.logical_not(here))
            def _():
                result(m, n).start()
            return 0
        lax.fori_loop(0, 2, multiply, 0)

    for m in range(AHEAD3):
        turn0(m)

    def round3(k, _):
        @pl.when(k < NO - AHEAD3)
        def _():
            turn0(k + AHEAD3)

        @pl.when(jnp.logical_and(k >= 1, k < NO + 1))
        def _():
            turn1(k - 1)

        @pl.when(jnp.logical_and(k >= 2, k < NO + 2))
        def _():
            turn2(k - 2)

        @pl.when(jnp.logical_and(k >= 3, k < NO + 3))
        def _():
            turn3(k - 3)

        @pl.when(k == 1)
        def _():
            for copy in o_third_in():
                copy.wait_recv()

        @pl.when(jnp.logical_and(k >= 1, k < 5))
        def _():
            for i in range(4):
                for copy in o_fourth(4 * k - 4 + i):
                    copy.start()

        @pl.when(k == FULL)
        def _():
            for copy in o_fourth_in():
                copy.wait_recv()

        def done3(k_):
            return jnp.maximum(jnp.minimum(k_ - 3, 2 * (k_ - FULL + 1)), 0)

        def multiply(m, _):
            turn4(m)
            return 0
        lax.fori_loop(done3(k - 1), done3(k), multiply, 0)
        return 0
    lax.fori_loop(0, NO + 4, round3, 0)

    def sent1(r, _):
        part = xg.at[0, pl.ds(0, 15), pl.ds(0, CH)]
        pltpu.make_async_copy(part, part, g_s.at[r]).wait()
        return 0
    lax.fori_loop(0, NC, sent1, 0)

    def sent3(m, _):
        part = ag.at[m, pl.ds(0, 15)]
        pltpu.make_async_copy(part, part, a_s.at[m]).wait()
        return 0
    lax.fori_loop(0, NO, sent3, 0)

    def sent_result(m, _):
        for n in range(2):
            @pl.when(jnp.logical_not(jnp.logical_and(mine, n == xi)))
            def _(n=n):
                result(m, n).wait_send()
        return 0
    lax.fori_loop(0, NO, sent_result, 0)

    @pl.when(other)
    def _():
        for r in range(NC):
            tok_remote(r).wait_send()
        for d in range(2):
            w_wait(1024, w2_s.at[d])
            w_wait(512, w3_s.at[d])

    @pl.when(mine)
    def _():
        w_wait(1024, w1_s.at[0])
    for copy in [o_first(d) for d in (1, 2, 3)] + [o_part(k, x, xn, 0, 1024) for k in range(3)] + o_third_out() + o_fourth_out():
        copy.wait_send()

    def sent_state(to, _):
        state_copy(to).wait_send()
        return 0
    lax.fori_loop(shard + 1, 8, sent_state, 0)

    pltpu.make_async_copy(tok, out, r_r.at[0]).wait()


def local(scale, tokens, w_query, w_key, w_value, w_output):
    rows, feat = tokens.shape
    wide = w_query.shape[0]
    dma, vmem = pltpu.SemaphoreType.DMA, pltpu.VMEM
    return pl.pallas_call(
        lambda *refs: kernel(scale, *refs),
        out_shape=jax.ShapeDtypeStruct((rows, feat), BF),
        in_specs=[pl.BlockSpec(memory_space=pl.ANY)] * 5,
        out_specs=pl.BlockSpec(memory_space=pl.ANY),
        scratch_shapes=[
            vmem((NB, 16, BLOCK, FEAT), BF),
            vmem((3, wide, FEAT), BF),
            vmem((NB, BLOCK, FEAT), BF),
            vmem((3, BLOCK, FEAT), BF),
            vmem((NB, BLOCK, FEAT), F32),
            vmem((NB, 2, DH, DH), F32),
            vmem((2, DH, DH), F32),
            vmem((2, DH, DH), BF),
            vmem((8, 2, DH, DH), BF),
            vmem((NB, 2, DH, DH), BF),
            vmem((NO, OC, FEAT), BF),
            vmem((NO, 16, OC, FEAT), BF),
            vmem((2, wide, FEAT), BF),
            vmem((NO, 2, OC, FEAT), BF),
            dma((NC,)), dma((NC,)),
            dma((3,)),
            dma((1,)), dma((8,)),
            dma((2,)), dma((2, 8)),
            dma((2,)), dma((2,)),
            dma((4,)), dma((4,)),
            dma((3,)), dma((3, 16)),
            dma((4,)), dma((4,)),
            dma((NC,)), dma((NC, 16)),
            dma((8,)), dma((8,)),
            dma((NO,)), dma((NO, 8)),
            dma((NO, 2)), dma((1,)),
        ],
        name="layer",
        cost_estimate=pl.CostEstimate(flops=18_000_000_000, bytes_accessed=12 << 20, transcendentals=0),
        compiler_params=pltpu.CompilerParams(
            collective_id=0, has_side_effects=True, vmem_limit_bytes=56 << 20),
    )(tokens, w_query, w_key, w_value, w_output)


def solution(mesh):
    scale = 1.0 / math.sqrt(DH * 16384)
    in_specs = (
        P("seq", "tensor"),
        P(None, "tensor"),
        P(None, "tensor"),
        P(None, "tensor"),
        P("tensor", None),
    )
    return jax.shard_map(
        lambda *args: local(scale, *args),
        mesh=mesh, in_specs=in_specs, out_specs=P("seq", "tensor"), check_vma=False)
```

```python
import math

import jax
import jax.numpy as jnp
from jax import lax
from jax.experimental import pallas as pl
from jax.experimental.pallas import tpu as pltpu
from jax.sharding import PartitionSpec as P

DH = 128
BLOCK = 256
BF = jnp.bfloat16
F32 = jnp.float32
NB = 8
CH = 128
NC = 16
RX = 80
RZ = CH - RX
HZ = 32
OC = 128
NO = 8
FEAT = 256
SIB = 15
SIB3 = 7
AHEAD = 0
WP = 128
FULL = 6
OP = 64
THIRD = 12
LATE = 12
AHEAD3 = 1


def remote(src, dst, send, recv, device):
    return pltpu.make_async_remote_copy(
        src_ref=src, dst_ref=dst, send_sem=send, recv_sem=recv,
        device_id=device, device_id_type=pl.DeviceIdType.MESH,
    )


def wide_rows(gathered, index):
    return jnp.concatenate([gathered[index, p] for p in range(16)], axis=1)


def kernel(scale, tok, wq, wk, wv, wo, out,
           xg, w, q, qkv, intra, st, run, tot, carry, low, attn, ag, wog, outb,
           pre_s, pre_r, w_l, w1_s, w1_r, w2_s, w2_r, w3_s, w3_r, o1_s, o1_r, o2_s, o2_r, o3_s, o3_r,
           g_s, g_r, t_s, t_r, a_s, a_r, r_s, r_r):
    div, rem = lax.div, lax.rem
    seq, ten = lax.axis_index("seq"), lax.axis_index("tensor")
    y, c, x, z = div(seq, 2), rem(seq, 2), div(ten, 4), rem(ten, 4)
    half, xi = div(x, 2), rem(x, 2)
    xn, xc = x + 1 - 2 * xi, 3 - x
    xd = 3 - xn
    mine = c == half
    other = jnp.logical_not(mine)
    shard = 2 * y + half
    zp, zm, z2 = rem(z + 1, 4), rem(z + 3, 4), rem(z + 2, 4)

    def at(y_, c_, x_, z_):
        return (2 * y_ + c_, 4 * x_ + z_)

    d_xn, d_zp, d_zm = at(y, c, xn, z), at(y, c, x, zp), at(y, c, x, zm)
    d_sib, d_part = at(y, 1 - c, x, z), at(y, 1 - c, xc, z)

    def col(x_, z_):
        return jnp.where(mine, x_, 3 - x_) * 4 + z_

    places = ((x, z), (xn, z), (x, zm), (x, zp), (xn, zm), (xn, zp), (x, z2), (xn, z2))
    cols = [col(*p) for p in places]
    c_own, c_x, c_m, c_p, c_xm, c_xp, c_2, c_x2 = cols

    barrier = pltpu.get_barrier_semaphore()
    peers = [d_sib, d_part, at(y, 1 - c, xd, z)]
    for d in (1, 2, 3):
        peers += [at(y, c, x, rem(z + d, 4)), at(y, c, rem(x + d, 4), z),
                  at(rem(y + d, 4), c, x, z), at(rem(y + d, 4), c, xc, z)]
    for peer in peers:
        pl.semaphore_signal(barrier, inc=1, device_id=peer, device_id_type=pl.DeviceIdType.MESH)

    w_hbm = (wq, wk, wv)
    quarter = pl.ds(pl.multiple_of(y * 1024, 1024), 1024)

    def tok_rows(r):
        return tok.at[pl.ds(pl.multiple_of(r * CH, CH), CH)]

    def slot(r, piece, first=0, count=CH):
        rows = pl.ds(pl.multiple_of(rem(r, 2) * CH + first, 16), count)
        return xg.at[div(r, 2), piece, rows]

    def tok_local(r):
        return pltpu.make_async_copy(tok_rows(r), slot(r, ten), pre_r.at[r])

    def tok_remote(r):
        return remote(tok_rows(r), slot(r, ten), pre_s.at[r], pre_r.at[r], d_part)

    def tok_wait(r):
        pltpu.make_async_copy(tok_rows(r), slot(r, c_own), pre_r.at[r]).wait()

    def w_local(n):
        return pltpu.make_async_copy(w_hbm[n], w.at[n], w_l.at[n])

    def w_rows(y_, i, first=0, count=WP):
        return pl.ds(pl.multiple_of(y_ * 1024 + i * WP + first, 16), count)

    def w_first(n, i):
        rows = w_rows(y, i)
        return remote(w_hbm[n].at[rows], w.at[n, rows], w1_s.at[0], w1_r.at[i], at(y, c, xc, z))

    yp, ym, y2 = rem(y + 1, 4), rem(y + 3, 4), rem(y + 2, 4)
    d_yp, d_ym = at(yp, c, x, z), at(ym, c, x, z)

    def w_second(n, i):
        part = w.at[n, w_rows(y, i)]
        return [remote(part, part, w2_s.at[k], w2_r.at[k, i], to) for k, to in enumerate((d_yp, d_ym))]

    def w_third(n, i):
        parts = w.at[n, w_rows(ym, i, 0, WP // 2)], w.at[n, w_rows(yp, i, WP // 2, WP // 2)]
        return [remote(part, part, w3_s.at[k], w3_r.at[k], to) for k, (part, to) in enumerate(zip(parts, (d_yp, d_ym)))]

    def w_wait(rows, semaphore):
        part = w.at[:, pl.ds(0, rows)]
        pltpu.make_async_copy(part, part, semaphore).wait()

    o_cols = pl.ds(pl.multiple_of(rem(y, 2) * DH, DH), DH)
    o_blk = div(y, 2)

    def o_source(z_):
        return wo.at[:, pl.ds(pl.multiple_of(((2 * c + o_blk) * 4 + z_) * FEAT + rem(y, 2) * DH, DH), DH)]

    o_mine = wog.at[o_blk, pl.ds(pl.multiple_of(ten * FEAT, FEAT), FEAT), o_cols]

    def o_first(d):
        if d == 0:
            return pltpu.make_async_copy(o_source(z), o_mine, o1_r.at[0])
        to = rem(z + d, 4)
        return remote(o_source(to), o_mine, o1_s.at[d], o1_r.at[d], at(y, c, x, to))

    def o_part(k, x_, to, i, count=OP):
        rows = pl.ds(pl.multiple_of(x_ * 1024 + i * OP, OP), count)
        part = wog.at[o_blk, rows, o_cols]
        return remote(part, part, o2_s.at[k], o2_r.at[k, i], at(y, c, to, z))

    def o_copy(k, y_, first, count, device=None):
        rows, columns = pl.ds(pl.multiple_of(first, 16), count), pl.ds(pl.multiple_of(rem(y_, 2) * DH, DH), DH)
        part = wog.at[div(y_, 2), rows, columns]
        return remote(part, part, o3_s.at[k], o3_r.at[k], d_yp if device is None else device)

    def o_third(x_, i):
        first = x_ * 1024 + i * WP
        return [o_copy(0, y, first, WP, d_yp), o_copy(1, y, first, WP, d_ym)]

    def o_third_out():
        return [o_copy(0, y, 0, 4096, d_yp), o_copy(1, y, 0, 4096, d_ym)]

    def o_third_in():
        return [o_copy(0, ym, 0, 4096), o_copy(1, yp, 0, 4096)]

    def o_fourth(i):
        return [o_copy(2, ym, i * WP, WP, d_yp), o_copy(3, yp, 2048 + i * WP, WP, d_ym)]

    def o_fourth_out():
        return [o_copy(2, ym, 0, 2048), o_copy(3, yp, 2048, 2048)]

    def o_fourth_in():
        return [o_copy(2, y2, 0, 2048), o_copy(3, y2, 2048, 2048)]

    @pl.when(mine)
    def _():
        def start(r, _):
            tok_local(r).start()
            return 0
        lax.fori_loop(0, NC, start, 0)
        for n in (1, 2, 0):
            w_local(n).start()

    pl.semaphore_wait(barrier, len(peers))

    def send_inputs(k):
        @pl.when(jnp.logical_and(other, k == 0))
        def _():
            for r in range(4):
                tok_remote(r).start()

        @pl.when(jnp.logical_and(other, jnp.logical_and(k >= 1, k < NC - 3)))
        def _():
            tok_remote(k + 3).start()

        @pl.when(jnp.logical_and(mine, k < 8))
        def _():
            for n in (1, 2, 0):
                w_first(n, k).start()

        @pl.when(jnp.logical_and(other, jnp.logical_and(k >= 2, k < 10)))
        def _():
            w_wait(WP, w1_r.at[k - 2])
            for n in (1, 2, 0):
                for copy in w_second(n, k - 2):
                    copy.start()

        @pl.when(jnp.logical_and(other, jnp.logical_and(k >= 4, k < 12)))
        def _():
            for d in range(2):
                w_wait(WP, w2_r.at[d, k - 4])
            for n in (1, 2, 0):
                for copy in w_third(n, k - 4):
                    copy.start()

        @pl.when(k == 0)
        def _():
            for d in range(4):
                o_first(d).start()

        @pl.when(k == 2)
        def _():
            o_first(0).wait()
            for d in (1, 2, 3):
                o_first(d).wait_recv()

        def third(x_, i):
            for copy in o_third(x_, i):
                copy.start()

        @pl.when(jnp.logical_and(k >= 2, k < 18))
        def _():
            o_part(0, x, xn, k - 2).start()
            o_part(1, x, xc, k - 2).start()

        @pl.when(jnp.logical_and(k >= 4, k < 20))
        def _():
            o_part(0, xn, xn, k - 4).wait_recv()
            o_part(2, xn, xc, k - 4).start()

        @pl.when(k >= THIRD)
        def _():
            i = k - THIRD
            third(x, i)
            third(xn, i)
            for half_piece in range(2):
                o_part(1, xc, xn, 2 * i + half_piece).wait_recv()
            third(xc, i)

        @pl.when(k >= THIRD + 1)
        def _():
            third_last(k - THIRD - 1)

    def third(x_, i):
        for copy in o_third(x_, i):
            copy.start()

    def third_last(i):
        for half_piece in range(2):
            o_part(2, xd, xn, 2 * i + half_piece).wait_recv()
        third(xd, i)

    ALL, XF, ZF, Z1, Z2 = (0, CH), (0, RX), (RX, RZ), (RX, HZ), (RX + HZ, RZ - HZ)

    def gather(r, k, rows, column, device=None):
        part = slot(r, column, *rows)
        return remote(part, part, g_s.at[r], g_r.at[r, k], d_sib if device is None else device)

    def to_sibling(r, piece):
        gather(r, SIB, ALL, cols[piece]).start()

    c_long, c_short = jnp.where(c == 0, c_m, c_p), jnp.where(c == 0, c_p, c_m)
    d_long, d_short = at(y, c, x, jnp.where(c == 0, zp, zm)), at(y, c, x, jnp.where(c == 0, zm, zp))

    def hop0(r):
        tok_wait(r)
        gather(r, 0, XF, c_own, d_xn).start()
        gather(r, 8, ZF, c_own, d_zp).start()
        gather(r, 9, ZF, c_own, d_zm).start()
        gather(r, 1, XF, c_own, d_zp).start()
        gather(r, 2, XF, c_own, d_zm).start()
        gather(r, 7, ZF, c_own, d_xn).start()
        to_sibling(r, 0)

    def hop1(r):
        gather(r, 0, XF, c_x).wait_recv()
        gather(r, 3, XF, c_x, d_zp).start()
        gather(r, 4, XF, c_x, d_zm).start()
        gather(r, 8, ZF, c_m).wait_recv()
        gather(r, 12, ZF, c_m, d_xn).start()
        gather(r, 9, ZF, c_p).wait_recv()
        gather(r, 13, ZF, c_p, d_xn).start()
        gather(r, 10, Z1, c_long, d_long).start()
        gather(r, 11, Z2, c_short, d_short).start()
        gather(r, 1, XF, c_m).wait_recv()
        gather(r, 5, XF, c_m, d_zp).start()
        to_sibling(r, 2)
        gather(r, 2, XF, c_p).wait_recv()
        to_sibling(r, 3)
        gather(r, 7, ZF, c_x).wait_recv()
        to_sibling(r, 1)

    def hop2(r):
        gather(r, 4, XF, c_xp).wait_recv()
        gather(r, 6, XF, c_xp, d_zm).start()
        gather(r, 10, Z1, c_2).wait_recv()
        gather(r, 11, Z2, c_2).wait_recv()
        gather(r, 14, ZF, c_2, d_xn).start()
        gather(r, 3, XF, c_xm).wait_recv()
        gather(r, 12, ZF, c_xm).wait_recv()
        to_sibling(r, 4)
        gather(r, 13, ZF, c_xp).wait_recv()
        to_sibling(r, 5)

    def hop3(r):
        gather(r, 5, XF, c_2).wait_recv()
        to_sibling(r, 6)
        gather(r, 6, XF, c_x2).wait_recv()
        gather(r, 14, ZF, c_x2).wait_recv()
        to_sibling(r, 7)

    def heads(n):
        return slice(n * DH, (n + 1) * DH)

    def state_copy(to):
        to_y, to_half = div(to, 2), rem(to, 2)
        to_x = jnp.where(to_half == half, x, xc)
        return remote(tot, carry.at[shard], t_s.at[to], t_r.at[shard], at(to_y, c, to_x, z))

    def project(r, n):
        qkv[n] = jnp.dot(wide_rows(xg, r), w[n], preferred_element_type=F32).astype(BF)

    def step_key(r):
        for half_block in range(2):
            eight = xg.at[r, pl.ds(0, 4)]
            remote(eight, eight, g_s.at[2 * r], g_r.at[2 * r + half_block, SIB], d_sib).wait_recv()
        project(r, 1)

    def step_value(r):
        project(r, 2)
        for n in range(2):
            total = run[n]
            st[r, n] = total
            run[n] = total + lax.dot_general(
                qkv[1, :, heads(n)], qkv[2, :, heads(n)], (((0,), (0,)), ((), ())), preferred_element_type=F32)

        @pl.when(r == NB - 1)
        def _():
            tot[...] = run[...].astype(BF)

            def send(to, _):
                state_copy(to).start()
                return 0
            lax.fori_loop(shard + 1, 8, send, 0)

    def step_query(r):
        project(r, 0)
        q[r] = qkv[0]

    def step_attend(r):
        causal = (lax.broadcasted_iota(jnp.int32, (BLOCK, BLOCK), 0)
                  >= lax.broadcasted_iota(jnp.int32, (BLOCK, BLOCK), 1))
        for n in range(2):
            scores = lax.dot_general(
                qkv[0, :, heads(n)], qkv[1, :, heads(n)], (((1,), (1,)), ((), ())), preferred_element_type=F32)
            scores = jnp.where(causal, scores, 0.0).astype(BF)
            intra[r, :, heads(n)] = jnp.dot(scores, qkv[2, :, heads(n)], preferred_element_type=F32)

    run[...] = jnp.zeros_like(run)

    send_inputs(0)
    for r in range(AHEAD):
        hop0(r)

    def done(k):
        return jnp.maximum(jnp.minimum(jnp.where(mine, NB, k - LATE + 1), div(k - 3, 2)), 0)

    def round1(k, _):
        block = done(k - 1)
        busy = done(k) > block

        @pl.when(k > 0)
        def _():
            send_inputs(k)

        @pl.when(k < NC - AHEAD)
        def _():
            hop0(k + AHEAD)

        @pl.when(jnp.logical_and(mine, k == 5))
        def _():
            for n in range(3):
                w_local(n).wait()

        @pl.when(jnp.logical_and(other, k == LATE))
        def _():
            for d in range(2):
                w_wait(512, w3_r.at[d])

        steps = (step_key, step_value, step_query, step_attend)
        for late, (hop, step) in enumerate(zip((None, hop1, hop2, hop3), steps)):
            if hop is not None:
                @pl.when(jnp.logical_and(k >= late, k < NC + late))
                def _(hop=hop, late=late):
                    hop(k - late)

            @pl.when(busy)
            def _(step=step):
                step(block)
        return 0
    lax.fori_loop(0, NC + 4, round1, 0)

    third_last(7)

    run[...] = jnp.zeros_like(run)

    def add(k, _):
        remote(tot, carry.at[k], t_s.at[k], t_r.at[k], d_sib).wait_recv()
        run[...] += carry[k].astype(F32)
        return 0
    lax.fori_loop(0, shard, add, 0)

    def lower(r, _):
        low[r] = (st[r] + run[...]).astype(BF)
        return 0
    lax.fori_loop(0, NB, lower, 0)

    def attended(r, first):
        rows = pl.ds(pl.multiple_of(first, OC), OC)
        parts = []
        for n in range(2):
            inter = jnp.dot(q[r, rows, heads(n)], low[r, n], preferred_element_type=F32)
            parts.append(((inter + intra[r, rows, heads(n)]) * scale).astype(BF))
        return jnp.concatenate(parts, axis=1)

    def slot3(m, piece):
        return ag.at[m, piece]

    def spread(m, k, column, device=None):
        part = slot3(m, column)
        return remote(part, part, a_s.at[m], a_r.at[m, k], d_sib if device is None else device)

    def spread_sibling(m, piece):
        spread(m, SIB3, cols[piece]).start()

    def hand_over(m):
        return remote(attn.at[m], slot3(m, c_own), a_s.at[m], a_r.at[m, 0], d_xn)

    def turn0(m):
        r, first = 2 * div(m, 2), rem(m, 2) * OC
        slot3(m, c_own)[...] = attended(r + xi, first)
        spread(m, 1, c_own, d_zp).start()
        spread(m, 2, c_own, d_zm).start()
        attn[m] = attended(r + 1 - xi, first)
        hand_over(m).start()
        spread_sibling(m, 0)

    def turn1(m):
        spread(m, 0, c_x).wait_recv()
        spread(m, 3, c_x, d_zp).start()
        spread(m, 4, c_x, d_zm).start()
        spread_sibling(m, 1)
        spread(m, 1, c_m).wait_recv()
        spread(m, 5, c_m, d_zp).start()
        spread_sibling(m, 2)
        spread(m, 2, c_p).wait_recv()
        spread_sibling(m, 3)

    def turn2(m):
        spread(m, 4, c_xp).wait_recv()
        spread(m, 6, c_xp, d_zm).start()
        spread_sibling(m, 5)
        spread(m, 3, c_xm).wait_recv()
        spread_sibling(m, 4)

    def turn3(m):
        spread(m, 5, c_2).wait_recv()
        spread_sibling(m, 6)
        spread(m, 6, c_x2).wait_recv()
        spread_sibling(m, 7)

    def out_rows(m):
        return pl.ds(pl.multiple_of((2 * div(m, 2) + xi) * BLOCK + rem(m, 2) * OC, OC), OC)

    def result(m, n):
        return remote(outb.at[m, n], out.at[out_rows(m)], r_s.at[m, n], r_r.at[0],
                      at(y, half, 2 * c + n, z))

    def result_local(m, n):
        return pltpu.make_async_copy(outb.at[m, n], out.at[out_rows(m)], r_r.at[0])

    def turn4(m):
        eight = ag.at[m, pl.ds(0, 8)]
        remote(eight, eight, a_s.at[m], a_r.at[m, SIB3], d_sib).wait_recv()

        def multiply(n, _):
            outb[m, n] = jnp.dot(wide_rows(ag, m), wog[n], preferred_element_type=F32).astype(BF)
            here = jnp.logical_and(mine, n == xi)

            @pl.when(here)
            def _():
                result_local(m, n).start()

            @pl.when(jnp.logical_not(here))
            def _():
                result(m, n).start()
            return 0
        lax.fori_loop(0, 2, multiply, 0)

    for m in range(AHEAD3):
        turn0(m)

    def round3(k, _):
        @pl.when(k < NO - AHEAD3)
        def _():
            turn0(k + AHEAD3)

        @pl.when(jnp.logical_and(k >= 1, k < NO + 1))
        def _():
            turn1(k - 1)

        @pl.when(jnp.logical_and(k >= 2, k < NO + 2))
        def _():
            turn2(k - 2)

        @pl.when(jnp.logical_and(k >= 3, k < NO + 3))
        def _():
            turn3(k - 3)

        @pl.when(k == 1)
        def _():
            for copy in o_third_in():
                copy.wait_recv()

        @pl.when(jnp.logical_and(k >= 1, k < 5))
        def _():
            for i in range(4):
                for copy in o_fourth(4 * k - 4 + i):
                    copy.start()

        @pl.when(k == FULL)
        def _():
            for copy in o_fourth_in():
                copy.wait_recv()

        def done3(k_):
            return jnp.maximum(jnp.minimum(k_ - 3, 2 * (k_ - FULL + 1)), 0)

        def multiply(m, _):
            turn4(m)
            return 0
        lax.fori_loop(done3(k - 1), done3(k), multiply, 0)
        return 0
    lax.fori_loop(0, NO + 4, round3, 0)

    def sent1(r, _):
        part = xg.at[0, pl.ds(0, 15), pl.ds(0, CH)]
        pltpu.make_async_copy(part, part, g_s.at[r]).wait()
        return 0
    lax.fori_loop(0, NC, sent1, 0)

    def sent3(m, _):
        part = ag.at[m, pl.ds(0, 15)]
        pltpu.make_async_copy(part, part, a_s.at[m]).wait()
        return 0
    lax.fori_loop(0, NO, sent3, 0)

    def sent_result(m, _):
        for n in range(2):
            @pl.when(jnp.logical_not(jnp.logical_and(mine, n == xi)))
            def _(n=n):
                result(m, n).wait_send()
        return 0
    lax.fori_loop(0, NO, sent_result, 0)

    @pl.when(other)
    def _():
        for r in range(NC):
            tok_remote(r).wait_send()
        for d in range(2):
            w_wait(1024, w2_s.at[d])
            w_wait(512, w3_s.at[d])

    @pl.when(mine)
    def _():
        w_wait(1024, w1_s.at[0])
    for copy in [o_first(d) for d in (1, 2, 3)] + [o_part(k, x, xn, 0, 1024) for k in range(3)] + o_third_out() + o_fourth_out():
        copy.wait_send()

    def sent_state(to, _):
        state_copy(to).wait_send()
        return 0
    lax.fori_loop(shard + 1, 8, sent_state, 0)

    pltpu.make_async_copy(tok, out, r_r.at[0]).wait()


def local(scale, tokens, w_query, w_key, w_value, w_output):
    rows, feat = tokens.shape
    wide = w_query.shape[0]
    dma, vmem = pltpu.SemaphoreType.DMA, pltpu.VMEM
    return pl.pallas_call(
        lambda *refs: kernel(scale, *refs),
        out_shape=jax.ShapeDtypeStruct((rows, feat), BF),
        in_specs=[pl.BlockSpec(memory_space=pl.ANY)] * 5,
        out_specs=pl.BlockSpec(memory_space=pl.ANY),
        scratch_shapes=[
            vmem((NB, 16, BLOCK, FEAT), BF),
            vmem((3, wide, FEAT), BF),
            vmem((NB, BLOCK, FEAT), BF),
            vmem((3, BLOCK, FEAT), BF),
            vmem((NB, BLOCK, FEAT), F32),
            vmem((NB, 2, DH, DH), F32),
            vmem((2, DH, DH), F32),
            vmem((2, DH, DH), BF),
            vmem((8, 2, DH, DH), BF),
            vmem((NB, 2, DH, DH), BF),
            vmem((NO, OC, FEAT), BF),
            vmem((NO, 16, OC, FEAT), BF),
            vmem((2, wide, FEAT), BF),
            vmem((NO, 2, OC, FEAT), BF),
            dma((NC,)), dma((NC,)),
            dma((3,)),
            dma((1,)), dma((8,)),
            dma((2,)), dma((2, 8)),
            dma((2,)), dma((2,)),
            dma((4,)), dma((4,)),
            dma((3,)), dma((3, 16)),
            dma((4,)), dma((4,)),
            dma((NC,)), dma((NC, 16)),
            dma((8,)), dma((8,)),
            dma((NO,)), dma((NO, 8)),
            dma((NO, 2)), dma((1,)),
        ],
        name="layer",
        cost_estimate=pl.CostEstimate(flops=18_000_000_000, bytes_accessed=12 << 20, transcendentals=0),
        compiler_params=pltpu.CompilerParams(
            collective_id=0, has_side_effects=True, vmem_limit_bytes=56 << 20),
    )(tokens, w_query, w_key, w_value, w_output)


def solution(mesh):
    scale = 1.0 / math.sqrt(DH * 16384)
    in_specs = (
        P("seq", "tensor"),
        P(None, "tensor"),
        P(None, "tensor"),
        P(None, "tensor"),
        P("tensor", None),
    )
    return jax.shard_map(
        lambda *args: local(scale, *args),
        mesh=mesh, in_specs=in_specs, out_specs=P("seq", "tensor"), check_vma=False)
```

```python
import math

import jax
import jax.numpy as jnp
from jax import lax
from jax.experimental import pallas as pl
from jax.experimental.pallas import tpu as pltpu
from jax.sharding import PartitionSpec as P

DH = 128
BLOCK = 256
BF = jnp.bfloat16
F32 = jnp.float32
NB = 8
CH = 128
NC = 16
RX = 80
RZ = CH - RX
HZ = 32
OC = 128
NO = 8
FEAT = 256
SIB = 15
SIB3 = 7
AHEAD = 0
WP = 128
FULL = 7
OP = 64
THIRD = 12
LATE = 12
AHEAD3 = 1


def remote(src, dst, send, recv, device):
    return pltpu.make_async_remote_copy(
        src_ref=src, dst_ref=dst, send_sem=send, recv_sem=recv,
        device_id=device, device_id_type=pl.DeviceIdType.MESH,
    )


def wide_rows(gathered, index):
    return jnp.concatenate([gathered[index, p] for p in range(16)], axis=1)


def kernel(scale, tok, wq, wk, wv, wo, out,
           xg, w, q, qkv, intra, st, run, tot, carry, low, attn, ag, wog, outb,
           pre_s, pre_r, w_l, w1_s, w1_r, w2_s, w2_r, w3_s, w3_r, o1_s, o1_r, o2_s, o2_r, o3_s, o3_r,
           g_s, g_r, t_s, t_r, a_s, a_r, r_s, r_r):
    div, rem = lax.div, lax.rem
    seq, ten = lax.axis_index("seq"), lax.axis_index("tensor")
    y, c, x, z = div(seq, 2), rem(seq, 2), div(ten, 4), rem(ten, 4)
    half, xi = div(x, 2), rem(x, 2)
    xn, xc = x + 1 - 2 * xi, 3 - x
    xd = 3 - xn
    mine = c == half
    other = jnp.logical_not(mine)
    shard = 2 * y + half
    zp, zm, z2 = rem(z + 1, 4), rem(z + 3, 4), rem(z + 2, 4)

    def at(y_, c_, x_, z_):
        return (2 * y_ + c_, 4 * x_ + z_)

    d_xn, d_zp, d_zm = at(y, c, xn, z), at(y, c, x, zp), at(y, c, x, zm)
    d_sib, d_part = at(y, 1 - c, x, z), at(y, 1 - c, xc, z)

    def col(x_, z_):
        return jnp.where(mine, x_, 3 - x_) * 4 + z_

    places = ((x, z), (xn, z), (x, zm), (x, zp), (xn, zm), (xn, zp), (x, z2), (xn, z2))
    cols = [col(*p) for p in places]
    c_own, c_x, c_m, c_p, c_xm, c_xp, c_2, c_x2 = cols

    barrier = pltpu.get_barrier_semaphore()
    peers = [d_sib, d_part, at(y, 1 - c, xd, z)]
    for d in (1, 2, 3):
        peers += [at(y, c, x, rem(z + d, 4)), at(y, c, rem(x + d, 4), z),
                  at(rem(y + d, 4), c, x, z), at(rem(y + d, 4), c, xc, z)]
    for peer in peers:
        pl.semaphore_signal(barrier, inc=1, device_id=peer, device_id_type=pl.DeviceIdType.MESH)

    w_hbm = (wq, wk, wv)
    quarter = pl.ds(pl.multiple_of(y * 1024, 1024), 1024)

    def tok_rows(r):
        return tok.at[pl.ds(pl.multiple_of(r * CH, CH), CH)]

    def slot(r, piece, first=0, count=CH):
        rows = pl.ds(pl.multiple_of(rem(r, 2) * CH + first, 16), count)
        return xg.at[div(r, 2), piece, rows]

    def tok_local(r):
        return pltpu.make_async_copy(tok_rows(r), slot(r, ten), pre_r.at[r])

    def tok_remote(r):
        return remote(tok_rows(r), slot(r, ten), pre_s.at[r], pre_r.at[r], d_part)

    def tok_wait(r):
        pltpu.make_async_copy(tok_rows(r), slot(r, c_own), pre_r.at[r]).wait()

    def w_local(n):
        return pltpu.make_async_copy(w_hbm[n], w.at[n], w_l.at[n])

    def w_rows(y_, i, first=0, count=WP):
        return pl.ds(pl.multiple_of(y_ * 1024 + i * WP + first, 16), count)

    def w_first(n, i):
        rows = w_rows(y, i)
        return remote(w_hbm[n].at[rows], w.at[n, rows], w1_s.at[0], w1_r.at[i], at(y, c, xc, z))

    yp, ym, y2 = rem(y + 1, 4), rem(y + 3, 4), rem(y + 2, 4)
    d_yp, d_ym = at(yp, c, x, z), at(ym, c, x, z)

    def w_second(n, i):
        part = w.at[n, w_rows(y, i)]
        return [remote(part, part, w2_s.at[k], w2_r.at[k, i], to) for k, to in enumerate((d_yp, d_ym))]

    def w_third(n, i):
        parts = w.at[n, w_rows(ym, i, 0, WP // 2)], w.at[n, w_rows(yp, i, WP // 2, WP // 2)]
        return [remote(part, part, w3_s.at[k], w3_r.at[k], to) for k, (part, to) in enumerate(zip(parts, (d_yp, d_ym)))]

    def w_wait(rows, semaphore):
        part = w.at[:, pl.ds(0, rows)]
        pltpu.make_async_copy(part, part, semaphore).wait()

    o_cols = pl.ds(pl.multiple_of(rem(y, 2) * DH, DH), DH)
    o_blk = div(y, 2)

    def o_source(z_):
        return wo.at[:, pl.ds(pl.multiple_of(((2 * c + o_blk) * 4 + z_) * FEAT + rem(y, 2) * DH, DH), DH)]

    o_mine = wog.at[o_blk, pl.ds(pl.multiple_of(ten * FEAT, FEAT), FEAT), o_cols]

    def o_first(d):
        if d == 0:
            return pltpu.make_async_copy(o_source(z), o_mine, o1_r.at[0])
        to = rem(z + d, 4)
        return remote(o_source(to), o_mine, o1_s.at[d], o1_r.at[d], at(y, c, x, to))

    def o_part(k, x_, to, i, count=OP):
        rows = pl.ds(pl.multiple_of(x_ * 1024 + i * OP, OP), count)
        part = wog.at[o_blk, rows, o_cols]
        return remote(part, part, o2_s.at[k], o2_r.at[k, i], at(y, c, to, z))

    def o_copy(k, y_, first, count, device=None):
        rows, columns = pl.ds(pl.multiple_of(first, 16), count), pl.ds(pl.multiple_of(rem(y_, 2) * DH, DH), DH)
        part = wog.at[div(y_, 2), rows, columns]
        return remote(part, part, o3_s.at[k], o3_r.at[k], d_yp if device is None else device)

    def o_third(x_, i):
        first = x_ * 1024 + i * WP
        return [o_copy(0, y, first, WP, d_yp), o_copy(1, y, first, WP, d_ym)]

    def o_third_out():
        return [o_copy(0, y, 0, 4096, d_yp), o_copy(1, y, 0, 4096, d_ym)]

    def o_third_in():
        return [o_copy(0, ym, 0, 4096), o_copy(1, yp, 0, 4096)]

    def o_fourth(i):
        return [o_copy(2, ym, i * WP, WP, d_yp), o_copy(3, yp, 2048 + i * WP, WP, d_ym)]

    def o_fourth_out():
        return [o_copy(2, ym, 0, 2048), o_copy(3, yp, 2048, 2048)]

    def o_fourth_in():
        return [o_copy(2, y2, 0, 2048), o_copy(3, y2, 2048, 2048)]

    @pl.when(mine)
    def _():
        def start(r, _):
            tok_local(r).start()
            return 0
        lax.fori_loop(0, NC, start, 0)
        for n in (1, 2, 0):
            w_local(n).start()

    pl.semaphore_wait(barrier, len(peers))

    def send_inputs(k):
        @pl.when(jnp.logical_and(other, k == 0))
        def _():
            for r in range(4):
                tok_remote(r).start()

        @pl.when(jnp.logical_and(other, jnp.logical_and(k >= 1, k < NC - 3)))
        def _():
            tok_remote(k + 3).start()

        @pl.when(jnp.logical_and(mine, k < 8))
        def _():
            for n in (1, 2, 0):
                w_first(n, k).start()

        @pl.when(jnp.logical_and(other, jnp.logical_and(k >= 2, k < 10)))
        def _():
            w_wait(WP, w1_r.at[k - 2])
            for n in (1, 2, 0):
                for copy in w_second(n, k - 2):
                    copy.start()

        @pl.when(jnp.logical_and(other, jnp.logical_and(k >= 4, k < 12)))
        def _():
            for d in range(2):
                w_wait(WP, w2_r.at[d, k - 4])
            for n in (1, 2, 0):
                for copy in w_third(n, k - 4):
                    copy.start()

        @pl.when(k == 0)
        def _():
            for d in range(4):
                o_first(d).start()

        @pl.when(k == 2)
        def _():
            o_first(0).wait()
            for d in (1, 2, 3):
                o_first(d).wait_recv()

        def third(x_, i):
            for copy in o_third(x_, i):
                copy.start()

        @pl.when(jnp.logical_and(k >= 2, k < 18))
        def _():
            o_part(0, x, xn, k - 2).start()
            o_part(1, x, xc, k - 2).start()

        @pl.when(jnp.logical_and(k >= 4, k < 20))
        def _():
            o_part(0, xn, xn, k - 4).wait_recv()
            o_part(2, xn, xc, k - 4).start()

        @pl.when(k >= THIRD)
        def _():
            i = k - THIRD
            third(x, i)
            third(xn, i)
            for half_piece in range(2):
                o_part(1, xc, xn, 2 * i + half_piece).wait_recv()
            third(xc, i)

        @pl.when(k >= THIRD + 1)
        def _():
            third_last(k - THIRD - 1)

    def third(x_, i):
        for copy in o_third(x_, i):
            copy.start()

    def third_last(i):
        for half_piece in range(2):
            o_part(2, xd, xn, 2 * i + half_piece).wait_recv()
        third(xd, i)

    ALL, XF, ZF, Z1, Z2 = (0, CH), (0, RX), (RX, RZ), (RX, HZ), (RX + HZ, RZ - HZ)

    def gather(r, k, rows, column, device=None):
        part = slot(r, column, *rows)
        return remote(part, part, g_s.at[r], g_r.at[r, k], d_sib if device is None else device)

    def to_sibling(r, piece):
        gather(r, SIB, ALL, cols[piece]).start()

    c_long, c_short = jnp.where(c == 0, c_m, c_p), jnp.where(c == 0, c_p, c_m)
    d_long, d_short = at(y, c, x, jnp.where(c == 0, zp, zm)), at(y, c, x, jnp.where(c == 0, zm, zp))

    def hop0(r):
        tok_wait(r)
        gather(r, 0, XF, c_own, d_xn).start()
        gather(r, 8, ZF, c_own, d_zp).start()
        gather(r, 9, ZF, c_own, d_zm).start()
        gather(r, 1, XF, c_own, d_zp).start()
        gather(r, 2, XF, c_own, d_zm).start()
        gather(r, 7, ZF, c_own, d_xn).start()
        to_sibling(r, 0)

    def hop1(r):
        gather(r, 0, XF, c_x).wait_recv()
        gather(r, 3, XF, c_x, d_zp).start()
        gather(r, 4, XF, c_x, d_zm).start()
        gather(r, 8, ZF, c_m).wait_recv()
        gather(r, 12, ZF, c_m, d_xn).start()
        gather(r, 9, ZF, c_p).wait_recv()
        gather(r, 13, ZF, c_p, d_xn).start()
        gather(r, 10, Z1, c_long, d_long).start()
        gather(r, 11, Z2, c_short, d_short).start()
        gather(r, 1, XF, c_m).wait_recv()
        gather(r, 5, XF, c_m, d_zp).start()
        to_sibling(r, 2)
        gather(r, 2, XF, c_p).wait_recv()
        to_sibling(r, 3)
        gather(r, 7, ZF, c_x).wait_recv()
        to_sibling(r, 1)

    def hop2(r):
        gather(r, 4, XF, c_xp).wait_recv()
        gather(r, 6, XF, c_xp, d_zm).start()
        gather(r, 10, Z1, c_2).wait_recv()
        gather(r, 11, Z2, c_2).wait_recv()
        gather(r, 14, ZF, c_2, d_xn).start()
        gather(r, 3, XF, c_xm).wait_recv()
        gather(r, 12, ZF, c_xm).wait_recv()
        to_sibling(r, 4)
        gather(r, 13, ZF, c_xp).wait_recv()
        to_sibling(r, 5)

    def hop3(r):
        gather(r, 5, XF, c_2).wait_recv()
        to_sibling(r, 6)
        gather(r, 6, XF, c_x2).wait_recv()
        gather(r, 14, ZF, c_x2).wait_recv()
        to_sibling(r, 7)

    def heads(n):
        return slice(n * DH, (n + 1) * DH)

    def state_copy(to):
        to_y, to_half = div(to, 2), rem(to, 2)
        to_x = jnp.where(to_half == half, x, xc)
        return remote(tot, carry.at[shard], t_s.at[to], t_r.at[shard], at(to_y, c, to_x, z))

    def project(r, n):
        qkv[n] = jnp.dot(wide_rows(xg, r), w[n], preferred_element_type=F32).astype(BF)

    def step_key(r):
        for half_block in range(2):
            eight = xg.at[r, pl.ds(0, 4)]
            remote(eight, eight, g_s.at[2 * r], g_r.at[2 * r + half_block, SIB], d_sib).wait_recv()
        project(r, 1)

    def step_value(r):
        project(r, 2)
        for n in range(2):
            total = run[n]
            st[r, n] = total
            run[n] = total + lax.dot_general(
                qkv[1, :, heads(n)], qkv[2, :, heads(n)], (((0,), (0,)), ((), ())), preferred_element_type=F32)

        @pl.when(r == NB - 1)
        def _():
            tot[...] = run[...].astype(BF)

            def send(to, _):
                state_copy(to).start()
                return 0
            lax.fori_loop(shard + 1, 8, send, 0)

    def step_query(r):
        project(r, 0)
        q[r] = qkv[0]

    def step_attend(r):
        causal = (lax.broadcasted_iota(jnp.int32, (BLOCK, BLOCK), 0)
                  >= lax.broadcasted_iota(jnp.int32, (BLOCK, BLOCK), 1))
        for n in range(2):
            scores = lax.dot_general(
                qkv[0, :, heads(n)], qkv[1, :, heads(n)], (((1,), (1,)), ((), ())), preferred_element_type=F32)
            scores = jnp.where(causal, scores, 0.0).astype(BF)
            intra[r, :, heads(n)] = jnp.dot(scores, qkv[2, :, heads(n)], preferred_element_type=F32)

    run[...] = jnp.zeros_like(run)

    send_inputs(0)
    for r in range(AHEAD):
        hop0(r)

    def done(k):
        return jnp.maximum(jnp.minimum(jnp.where(mine, NB, k - LATE + 1), div(k - 3, 2)), 0)

    def round1(k, _):
        block = done(k - 1)
        busy = done(k) > block

        @pl.when(k > 0)
        def _():
            send_inputs(k)

        @pl.when(k < NC - AHEAD)
        def _():
            hop0(k + AHEAD)

        @pl.when(jnp.logical_and(mine, k == 5))
        def _():
            for n in range(3):
                w_local(n).wait()

        @pl.when(jnp.logical_and(other, k == LATE))
        def _():
            for d in range(2):
                w_wait(512, w3_r.at[d])

        steps = (step_key, step_value, step_query, step_attend)
        for late, (hop, step) in enumerate(zip((None, hop1, hop2, hop3), steps)):
            if hop is not None:
                @pl.when(jnp.logical_and(k >= late, k < NC + late))
                def _(hop=hop, late=late):
                    hop(k - late)

            @pl.when(busy)
            def _(step=step):
                step(block)
        return 0
    lax.fori_loop(0, NC + 4, round1, 0)

    third_last(7)

    run[...] = jnp.zeros_like(run)

    def add(k, _):
        remote(tot, carry.at[k], t_s.at[k], t_r.at[k], d_sib).wait_recv()
        run[...] += carry[k].astype(F32)
        return 0
    lax.fori_loop(0, shard, add, 0)

    def lower(r, _):
        low[r] = (st[r] + run[...]).astype(BF)
        return 0
    lax.fori_loop(0, NB, lower, 0)

    def attended(r, first):
        rows = pl.ds(pl.multiple_of(first, OC), OC)
        parts = []
        for n in range(2):
            inter = jnp.dot(q[r, rows, heads(n)], low[r, n], preferred_element_type=F32)
            parts.append(((inter + intra[r, rows, heads(n)]) * scale).astype(BF))
        return jnp.concatenate(parts, axis=1)

    def slot3(m, piece):
        return ag.at[m, piece]

    def spread(m, k, column, device=None):
        part = slot3(m, column)
        return remote(part, part, a_s.at[m], a_r.at[m, k], d_sib if device is None else device)

    def spread_sibling(m, piece):
        spread(m, SIB3, cols[piece]).start()

    def hand_over(m):
        return remote(attn.at[m], slot3(m, c_own), a_s.at[m], a_r.at[m, 0], d_xn)

    def turn0(m):
        r, first = 2 * div(m, 2), rem(m, 2) * OC
        attn[m] = attended(r + 1 - xi, first)
        hand_over(m).start()
        slot3(m, c_own)[...] = attended(r + xi, first)
        spread(m, 1, c_own, d_zp).start()
        spread(m, 2, c_own, d_zm).start()
        spread_sibling(m, 0)

    def turn1(m):
        spread(m, 0, c_x).wait_recv()
        spread(m, 3, c_x, d_zp).start()
        spread(m, 4, c_x, d_zm).start()
        spread_sibling(m, 1)
        spread(m, 1, c_m).wait_recv()
        spread(m, 5, c_m, d_zp).start()
        spread_sibling(m, 2)
        spread(m, 2, c_p).wait_recv()
        spread_sibling(m, 3)

    def turn2(m):
        spread(m, 4, c_xp).wait_recv()
        spread(m, 6, c_xp, d_zm).start()
        spread_sibling(m, 5)
        spread(m, 3, c_xm).wait_recv()
        spread_sibling(m, 4)

    def turn3(m):
        spread(m, 5, c_2).wait_recv()
        spread_sibling(m, 6)
        spread(m, 6, c_x2).wait_recv()
        spread_sibling(m, 7)

    def out_rows(m):
        return pl.ds(pl.multiple_of((2 * div(m, 2) + xi) * BLOCK + rem(m, 2) * OC, OC), OC)

    def result(m, n):
        return remote(outb.at[m, n], out.at[out_rows(m)], r_s.at[m, n], r_r.at[0],
                      at(y, half, 2 * c + n, z))

    def result_local(m, n):
        return pltpu.make_async_copy(outb.at[m, n], out.at[out_rows(m)], r_r.at[0])

    def turn4(m):
        eight = ag.at[m, pl.ds(0, 8)]
        remote(eight, eight, a_s.at[m], a_r.at[m, SIB3], d_sib).wait_recv()

        def multiply(n, _):
            outb[m, n] = jnp.dot(wide_rows(ag, m), wog[n], preferred_element_type=F32).astype(BF)
            here = jnp.logical_and(mine, n == xi)

            @pl.when(here)
            def _():
                result_local(m, n).start()

            @pl.when(jnp.logical_not(here))
            def _():
                result(m, n).start()
            return 0
        lax.fori_loop(0, 2, multiply, 0)

    for m in range(AHEAD3):
        turn0(m)

    def round3(k, _):
        @pl.when(k < NO - AHEAD3)
        def _():
            turn0(k + AHEAD3)

        @pl.when(jnp.logical_and(k >= 1, k < NO + 1))
        def _():
            turn1(k - 1)

        @pl.when(jnp.logical_and(k >= 2, k < NO + 2))
        def _():
            turn2(k - 2)

        @pl.when(jnp.logical_and(k >= 3, k < NO + 3))
        def _():
            turn3(k - 3)

        @pl.when(k == 1)
        def _():
            for copy in o_third_in():
                copy.wait_recv()

        @pl.when(jnp.logical_and(k >= 1, k < 5))
        def _():
            for i in range(4):
                for copy in o_fourth(4 * k - 4 + i):
                    copy.start()

        @pl.when(k == FULL)
        def _():
            for copy in o_fourth_in():
                copy.wait_recv()

        def done3(k_):
            return jnp.maximum(jnp.minimum(k_ - 3, 2 * (k_ - FULL + 1)), 0)

        def multiply(m, _):
            turn4(m)
            return 0
        lax.fori_loop(done3(k - 1), done3(k), multiply, 0)
        return 0
    lax.fori_loop(0, NO + 4, round3, 0)

    def sent1(r, _):
        part = xg.at[0, pl.ds(0, 15), pl.ds(0, CH)]
        pltpu.make_async_copy(part, part, g_s.at[r]).wait()
        return 0
    lax.fori_loop(0, NC, sent1, 0)

    def sent3(m, _):
        part = ag.at[m, pl.ds(0, 15)]
        pltpu.make_async_copy(part, part, a_s.at[m]).wait()
        return 0
    lax.fori_loop(0, NO, sent3, 0)

    def sent_result(m, _):
        for n in range(2):
            @pl.when(jnp.logical_not(jnp.logical_and(mine, n == xi)))
            def _(n=n):
                result(m, n).wait_send()
        return 0
    lax.fori_loop(0, NO, sent_result, 0)

    @pl.when(other)
    def _():
        for r in range(NC):
            tok_remote(r).wait_send()
        for d in range(2):
            w_wait(1024, w2_s.at[d])
            w_wait(512, w3_s.at[d])

    @pl.when(mine)
    def _():
        w_wait(1024, w1_s.at[0])
    for copy in [o_first(d) for d in (1, 2, 3)] + [o_part(k, x, xn, 0, 1024) for k in range(3)] + o_third_out() + o_fourth_out():
        copy.wait_send()

    def sent_state(to, _):
        state_copy(to).wait_send()
        return 0
    lax.fori_loop(shard + 1, 8, sent_state, 0)

    pltpu.make_async_copy(tok, out, r_r.at[0]).wait()


def local(scale, tokens, w_query, w_key, w_value, w_output):
    rows, feat = tokens.shape
    wide = w_query.shape[0]
    dma, vmem = pltpu.SemaphoreType.DMA, pltpu.VMEM
    return pl.pallas_call(
        lambda *refs: kernel(scale, *refs),
        out_shape=jax.ShapeDtypeStruct((rows, feat), BF),
        in_specs=[pl.BlockSpec(memory_space=pl.ANY)] * 5,
        out_specs=pl.BlockSpec(memory_space=pl.ANY),
        scratch_shapes=[
            vmem((NB, 16, BLOCK, FEAT), BF),
            vmem((3, wide, FEAT), BF),
            vmem((NB, BLOCK, FEAT), BF),
            vmem((3, BLOCK, FEAT), BF),
            vmem((NB, BLOCK, FEAT), F32),
            vmem((NB, 2, DH, DH), F32),
            vmem((2, DH, DH), F32),
            vmem((2, DH, DH), BF),
            vmem((8, 2, DH, DH), BF),
            vmem((NB, 2, DH, DH), BF),
            vmem((NO, OC, FEAT), BF),
            vmem((NO, 16, OC, FEAT), BF),
            vmem((2, wide, FEAT), BF),
            vmem((NO, 2, OC, FEAT), BF),
            dma((NC,)), dma((NC,)),
            dma((3,)),
            dma((1,)), dma((8,)),
            dma((2,)), dma((2, 8)),
            dma((2,)), dma((2,)),
            dma((4,)), dma((4,)),
            dma((3,)), dma((3, 16)),
            dma((4,)), dma((4,)),
            dma((NC,)), dma((NC, 16)),
            dma((8,)), dma((8,)),
            dma((NO,)), dma((NO, 8)),
            dma((NO, 2)), dma((1,)),
        ],
        name="layer",
        cost_estimate=pl.CostEstimate(flops=18_000_000_000, bytes_accessed=12 << 20, transcendentals=0),
        compiler_params=pltpu.CompilerParams(
            collective_id=0, has_side_effects=True, vmem_limit_bytes=56 << 20),
    )(tokens, w_query, w_key, w_value, w_output)


def solution(mesh):
    scale = 1.0 / math.sqrt(DH * 16384)
    in_specs = (
        P("seq", "tensor"),
        P(None, "tensor"),
        P(None, "tensor"),
        P(None, "tensor"),
        P("tensor", None),
    )
    return jax.shard_map(
        lambda *args: local(scale, *args),
        mesh=mesh, in_specs=in_specs, out_specs=P("seq", "tensor"), check_vma=False)
```
